32 devices in a mesh: dp: 8 (over z, y), mp: 4 (over x, core).
Axes of the slice: x: 2, y: 2, z: 4, core: 2. Of those that a mesh axis runs over, the one named last changes fastest.
Arguments:
- hidden_act: bfloat16 [2048, 14336], P('dp', 'mp'), may hold values from -6 to 6
- readout: bfloat16 [2048, 2560], P('dp'), may hold values from -6 to 6
- log_gap: float32 [256, 8], P('dp'), may hold values from -0.6 to 0.6
- advantage: float32 [256], P('dp'), may hold values from -6 to 6
- version: int32 [256], P('dp'), may hold values from 0 to 3
- lengths: int32 [8, 32], P('dp'), may hold values from 1 to 8, 224 in all within a row
- routes: int32 [256, 1], P('dp'), may hold values from 0 to 7; in each aligned block of 32 rows (0 to 31, 32 to 63, ...) at most 8 rows name the same one
- weight: bfloat16 [14336, 2560], P(('mp', 'dp')), may hold values from -0.046875 to 0.046875
Outputs:
- log_ratio: float32 [512, 8], P('dp')
- weight_grad: float32 [14336, 2560], P(('mp', 'dp'))
The draws below stay inside these ranges and needn't reach their ends.
Inputs may be any that keep to these rules, and one draw needn't show every extreme that they name: `routes`: among the 32 responses of one generator device at most 8 name the same learner shard, and some shard receives exactly 8; every learner shard receives at least one response. The lengths of one generator device's responses sum to 224, and one of them is 8.
All inputs are finite; a program needn't handle non-finite values.
Results may differ from the reference program's by a relative error of at most 0.0029.
Values may be sent and summed in bfloat16 or wider, within the bound.
No kernel may reach another device: no remote copies, remote signals or barrier semaphores. Data moves between devices by JAX's collectives and lax.ppermute only.
A program may use at most 128 MiB of HBM per device.

```python
import math
import jax
import jax.numpy as jnp
import numpy as np
from jax import lax

D = 2560
FF = 14336
SEG = 8
R = 32
NVER = 4
N_DP = 8


def plant(array, rng, least, high):
    longest = array.shape.index(max(array.shape))
    spots = []
    for shift in (0, 1):
        where = [jax.random.randint(jax.random.fold_in(rng, axis), (), 0, length) for axis, length in enumerate(array.shape)]
        where[longest] = (where[longest] + shift) % array.shape[longest]
        spots.append(tuple(where))
    return array.at[spots[0]].set(least).at[spots[1]].set(high)


def steps_of(rng, dims, split, smallest, largest):
    def one(dim, blocks):
        heights = jax.random.uniform(jax.random.fold_in(jax.random.fold_in(rng, 6), dim), (blocks,), jnp.float32, smallest / len(split), largest / len(split))
        return jnp.repeat(jnp.exp(heights), dims[dim] // blocks).reshape((-1,) + (1,) * (len(dims) - dim - 1))

    factor_of = one(*split[0])
    for cut in split[1:]:
        factor_of = factor_of * one(*cut)
    return factor_of


def length_profile(number_of, total, reach, lean):
    portions = [(1 << 20) // math.isqrt(rank ** lean) + 1 for rank in range(2, number_of + 1)]
    spare, given = total - reach - (number_of - 1), [1] * (number_of - 1)
    while spare > 0:
        free = [i for i in range(number_of - 1) if given[i] < reach]
        pool, remaining = sum([portions[i] for i in free]), spare
        for i in free:
            extra = min(reach - given[i], max(1, remaining * portions[i] // pool), spare)
            given[i] = given[i] + extra
            spare = spare - extra
    return np.array([reach] + given)


def ragged(key, amount, total, limit, skew):
    if amount == 2:
        one = jax.random.randint(key, (), max(1, total - limit), min(limit, total - 1) + 1)
        return jnp.stack([one, total - one])
    tallies = jnp.asarray(length_profile(amount, total, limit, skew), jnp.int32)
    twos = (amount - 1) // 2
    giver, taker = tallies[1:1 + 2 * twos:2], tallies[2:2 + 2 * twos:2]
    margin = jnp.minimum(giver - 1, limit - taker)
    shifted = jax.random.randint(jax.random.fold_in(key, 1), (twos,), 0, 1 << 20) % (margin + 1)
    tallies = tallies.at[1:1 + 2 * twos:2].set(giver - shifted).at[2:2 + 2 * twos:2].set(taker + shifted)
    return tallies[jax.random.permutation(jax.random.fold_in(key, 2), amount)]


def deal_out(key, own, number, rows, count, top, bound, lean):
    sequence = jax.random.permutation(key, count)
    heavy_load, ordinary = load_shares(count, rows * top, bound, lean, True), load_shares(count, rows * top, bound, lean, False)
    places = jnp.arange(count)

    def named(sizes, turn):
        used = int((sizes > 0).sum())
        fixed = max(1, used // 4)
        moved = fixed + (places - fixed + turn * (used - fixed)) % max(1, count - fixed)
        return jnp.zeros((count,), jnp.int32).at[sequence[jnp.where(places < fixed, places, moved)]].set(jnp.asarray(sizes, jnp.int32))

    sizes = jnp.where(number % 4 == 0, named(heavy_load, number // 4), named(ordinary, number - number // 4 - 1))
    mixed = jax.random.permutation(jax.random.fold_in(own, 3), count)
    donor, taker = mixed[0:count // 2 * 2:2], mixed[1:count // 2 * 2:2]
    margin = jnp.minimum(sizes[donor] - 1, bound - sizes[taker]) // 2
    margin = jnp.where((donor == sequence[0]) | (taker == sequence[0]) | (sizes[taker] == 0), 0, jnp.maximum(margin, 0))
    moved = jax.random.randint(jax.random.fold_in(own, 4), (count // 2,), 0, 1 << 20) % (margin + 1)
    sizes = sizes.at[donor].add(-moved).at[taker].add(moved)
    items = jnp.searchsorted(jnp.cumsum(sizes), jnp.arange(rows * top), side="right").astype(jnp.int32)
    table = items.reshape(top, rows).T
    table = table[jax.random.permutation(jax.random.fold_in(own, 1), rows)]
    turn = jax.random.randint(jax.random.fold_in(own, 2), (rows, 1), 0, top)
    return jnp.take_along_axis(table, (jnp.arange(top)[None, :] + turn) % top, axis=1)


def load_shares(number_of, total, reach, lean, full):
    portions = [(1 << 20) // math.isqrt(rank ** lean) + 1 for rank in range(1, number_of + 1)]
    largest = reach if full else min(reach, max(-(-total // number_of), total * portions[0] // sum(portions)))
    least = 1 if total - largest >= number_of - 1 else 0
    given, spare = [largest] + [least] * (number_of - 1), total - largest - least * (number_of - 1)
    while spare > 0:
        free = [i for i in range(1, number_of) if given[i] < largest] or [i for i in range(1, number_of) if given[i] < reach]
        pool, remaining = sum([portions[i] for i in free]), spare
        for i in free:
            addition = min(reach - given[i], max(1, remaining * portions[i] // pool), spare)
            given[i] = given[i] + addition
            spare = spare - addition
    return np.array(given)


def scatter_about(own_key, dims, deviation, most, split=(), kind=jnp.bfloat16):
    drawn = deviation * jax.random.normal(own_key, dims, jnp.float32)
    if split:
        drawn = drawn * steps_of(own_key, dims, split, -0.22, 0.18)
    return jnp.clip(drawn, -most, most).astype(kind)


def setup_inputs(seed: int = 0) -> dict:
    arg_keys = jax.random.split(jax.random.key(seed), 9)
    hidden_act = scatter_about(arg_keys[0], (N_DP * R * SEG, FF), 1.0, 6.0, ((0, 8), (1, 4)))
    readout = scatter_about(arg_keys[1], (N_DP * R * SEG, D), 1.0, 6.0, ((0, 8),))
    log_gap = scatter_about(arg_keys[2], (N_DP * R, SEG), 0.1, 0.6, ((0, 8),), jnp.float32)
    advantage = scatter_about(arg_keys[3], (N_DP * R,), 1.0, 6.0, ((0, 8),), jnp.float32)
    version = plant(jax.random.randint(arg_keys[4], (N_DP * R,), 0, NVER), jax.random.fold_in(arg_keys[4], 1), 0, NVER - 1).astype(jnp.int32)
    lengths = jax.vmap(lambda own: ragged(own, R, 7 * R * SEG // 8, SEG, 2))(jax.random.split(arg_keys[5], N_DP)).reshape((N_DP, R)).astype(jnp.int32)
    routes_keys = jax.random.split(jax.random.fold_in(arg_keys[6], 1), (N_DP * R) // R)
    routes_turns = jax.random.permutation(jax.random.fold_in(arg_keys[6], 3), (N_DP * R) // R)
    routes = jax.vmap(lambda own, number: deal_out(jax.random.fold_in(arg_keys[6], 2), own, number, R, N_DP, 1, 2 * R // N_DP, 2))(routes_keys, routes_turns).reshape((N_DP * R, 1))
    weight = scatter_about(arg_keys[7], (FF, D), FF ** -0.5, 0.046875, ((0, 32),))
    return {"hidden_act": hidden_act, "readout": readout, "log_gap": log_gap, "advantage": advantage, "version": version, "lengths": lengths, "routes": routes, "weight": weight}


def reference(hidden_act, readout, log_gap, advantage, version, lengths, routes, weight):
    slots = 2 * R // N_DP
    layer_out = jnp.dot(hidden_act, weight, preferred_element_type=jnp.float32)
    shift = 0.15 / math.sqrt(D) * lax.optimization_barrier(jnp.sum(layer_out * readout.astype(jnp.float32), axis=1))
    logit_all = log_gap + shift.reshape(N_DP * R, SEG)
    lens = lengths.reshape(-1)
    positions = jnp.arange(SEG, dtype=jnp.int32)
    live = positions[None, :] < lens[:, None]
    dest = routes[:, 0]
    onehot = (dest.reshape(N_DP, R)[:, :, None] == jnp.arange(N_DP, dtype=jnp.int32)[None, None, :]).astype(jnp.int32)
    rank = lax.optimization_barrier(jnp.sum((jnp.cumsum(onehot, axis=1) - onehot) * onehot, axis=2)).reshape(-1)
    source = jnp.arange(N_DP * R, dtype=jnp.int32) // R
    flat_hot = onehot.reshape(N_DP * R, N_DP).astype(jnp.float32)
    shard_count = lax.optimization_barrier(jnp.sum(flat_hot * lens.astype(jnp.float32)[:, None], axis=0))
    count_each = lax.optimization_barrier(jnp.sum(flat_hot * shard_count[None, :], axis=1))
    slot_index = ((dest * N_DP + source) * slots + rank).astype(jnp.int32)
    log_ratio = jnp.zeros((N_DP * N_DP * slots, SEG), jnp.float32).at[slot_index].set(jnp.where(live, logit_all, 0.0))
    stale = jnp.power(jnp.float32(0.7), (NVER - 1 - version).astype(jnp.float32))
    ratio = jnp.exp(logit_all)
    squash = jnp.tanh((ratio - 1.0) / 0.2)
    clipped = 1.0 + 0.2 * squash
    adv = advantage[:, None]
    plain = ratio * adv <= clipped * adv
    slope = jnp.where(plain, 1.0, 1.0 - squash * squash)
    coef = jnp.where(live, -512.0 * stale[:, None] * adv * ratio * slope / count_each[:, None], 0.0)
    out_grad = (coef.reshape(-1)[:, None] * (0.15 / math.sqrt(D)) * readout.astype(jnp.float32)).astype(jnp.bfloat16)
    weight_grad = lax.dot_general(hidden_act, out_grad, (((0,), (0,)), ((), ())), preferred_element_type=jnp.float32)
    return (log_ratio, weight_grad)
```

```python
import functools
import math

import jax
import jax.numpy as jnp
import numpy as np
from jax import lax
from jax.experimental import pallas as pl
from jax.experimental.pallas import tpu as pltpu
from jax.sharding import PartitionSpec as P

NVER = 4
SCALE = 0.15
EXACT = lax.Precision.HIGHEST
VMEM = pl.BlockSpec(memory_space=pltpu.VMEM)
SMEM = pl.BlockSpec(memory_space=pltpu.SMEM)
ANY = pl.BlockSpec(memory_space=pl.ANY)
GAP, ADV, STALE, DEST, RANK, POS = range(6)


def iota(shape, axis):
    return lax.broadcasted_iota(jnp.int32, shape, axis)


def rows_of(*rows):
    n = rows[0].shape[1]
    row = iota((8, n), 0)
    table = jnp.zeros((8, n), jnp.float32)
    for i, values in enumerate(rows):
        table = jnp.where(row == i, values, table)
    return table


def pack_readout(live_rows, seglen, place, lens, routes, gap, adv, version, read, table, sel, own, first, both):
    respond, tokens = gap.shape[0], gap.shape[0] * seglen
    mp = place[1]
    expand = (iota((respond, tokens), 0) == lax.div(iota((respond, tokens), 1), seglen)).astype(jnp.float32)
    spread = (iota((seglen, tokens), 0) == lax.rem(iota((seglen, tokens), 1), seglen)).astype(jnp.float32)
    eye = iota((respond, respond), 0) == iota((respond, respond), 1)
    dest_col = routes[...].astype(jnp.float32)
    dest_row = jnp.sum(jnp.where(eye, dest_col, 0.0), axis=0, keepdims=True)
    earlier = (dest_col == dest_row) & (iota((respond, respond), 0) < iota((respond, respond), 1))
    rank_row = jnp.sum(jnp.where(earlier, 1.0, 0.0), axis=0, keepdims=True)
    age = NVER - 1 - version[...]
    stale = jnp.ones(age.shape, jnp.float32)
    for years in range(1, NVER):
        stale = jnp.where(age == years, jnp.float32(np.float32(0.7) ** years), stale)
    by_token = jnp.dot(
        rows_of(adv[...], stale, dest_row, rank_row, lens[...].astype(jnp.float32)),
        expand, precision=EXACT, preferred_element_type=jnp.float32,
    )
    gap_wide = jnp.dot(gap[...], spread, precision=EXACT, preferred_element_type=jnp.float32)
    gap_row = jnp.sum(gap_wide * expand, axis=0, keepdims=True)
    pos_row = lax.rem(iota((1, tokens), 1), seglen).astype(jnp.float32)
    live = pos_row < by_token[4:5, :]
    before = (iota((tokens, tokens), 0) < iota((tokens, tokens), 1)).astype(jnp.bfloat16)
    live_wide = jnp.broadcast_to(live.astype(jnp.float32), (16, tokens)).astype(jnp.bfloat16)
    order = jnp.dot(live_wide, before, preferred_element_type=jnp.float32)[0:1, :]
    chosen = live & (order == iota((live_rows, tokens), 0).astype(jnp.float32))
    chosen_f32 = chosen.astype(jnp.float32)
    select = chosen_f32.astype(jnp.bfloat16)
    sel[...] = select
    table[...] = lax.dot_general(
        rows_of(gap_row, by_token[0:1, :], by_token[1:2, :], by_token[2:3, :], by_token[3:4, :], pos_row),
        chosen_f32, (((1,), (1,)), ((), ())), precision=EXACT, preferred_element_type=jnp.float32,
    )
    wide = read.shape[1] // 4
    for quarter in range(4):
        part = jnp.dot(
            select, read[:, quarter * wide:(quarter + 1) * wide], preferred_element_type=jnp.float32
        ).astype(jnp.bfloat16)
        own[mp ^ quarter] = part

        @pl.when(mp == quarter)
        def _():
            first[...] = part
            both[:live_rows] = part

        @pl.when((mp ^ 2) == quarter)
        def _():
            both[live_rows:] = part


def packed_rows(units, live_rows):
    return units * live_rows // 128


def pack_hidden(place, hidden, sel, *rest):
    outs, held = rest[:-1], rest[-1]
    dp = place[0]
    live_rows = sel.shape[0]
    units = hidden.shape[1] // len(outs)
    tail = live_rows - 128
    fold = 128 // math.gcd(tail, 128)
    short = units // fold
    pieces = tail * fold // 128
    rows = packed_rows(units, live_rows)
    for block in range(0, len(outs), 2):
        turned = lax.dot_general(
            hidden[:, block * units:(block + 2) * units], sel[...], (((0,), (1,)), ((), ())),
            preferred_element_type=jnp.float32,
        )
        for i in range(2):
            part = turned[i * units:(i + 1) * units]
            at = (block + i) * rows
            held[at:at + units] = part[:, :128].astype(jnp.bfloat16)
            wide = jnp.concatenate([part[j * short:(j + 1) * short, 128:] for j in range(fold)], axis=1)
            for j in range(pieces):
                start = at + units + j * short
                held[start:start + short] = wide[:, j * 128:(j + 1) * 128].astype(jnp.bfloat16)
    for k, out in enumerate(outs):
        out[...] = held[pl.ds(pl.multiple_of((dp ^ k) * rows, 16), rows)]


def unpack_hidden(packed, units, live_rows):
    tail = live_rows - 128
    fold = 128 // math.gcd(tail, 128)
    short = units // fold
    pieces = tail * fold // 128
    wide = jnp.concatenate(
        [packed[units + j * short:units + (j + 1) * short].astype(jnp.float32) for j in range(pieces)], axis=1
    )
    folded = jnp.concatenate([wide[:, j * tail:(j + 1) * tail] for j in range(fold)], axis=0)
    return packed[:units].astype(jnp.float32), folded


def fetch(pieces, refs, held, sems):
    copies = {}
    live_rows = held.shape[2]
    for (k, e), (ref, at) in pieces.items():
        source = refs[ref].at[at] if ref == 0 else refs[ref].at[pl.ds(at * live_rows, live_rows)]
        copy = pltpu.make_async_copy(source, held.at[e, k], sems.at[k, e])
        copy.start()
        copies[k, e] = copy
    return copies


def shift_kernel(pieces, n_refs, slots, place, weight, *rest):
    n = len(slots)
    hidden, refs, out = rest[:n], rest[n:n + n_refs], rest[n + n_refs]
    held, sems = rest[n + n_refs + 1:]
    mp = place[1]
    wide, live_rows = held.shape[3], held.shape[2]
    units = weight.shape[0]
    copies = fetch(pieces, refs, held, sems)
    row = iota((8, live_rows), 0)
    total = jnp.zeros((8, live_rows), jnp.float32)
    for i in range(n):
        product = jnp.zeros((units, live_rows), jnp.float32)
        for e in range(4):
            copies[i, e].wait()
            product += lax.dot_general(
                weight[:, pl.ds(pl.multiple_of((mp ^ e) * wide, 128), wide)], held[e, i],
                (((1,), (1,)), ((), ())), preferred_element_type=jnp.float32,
            )
        head, tail = unpack_hidden(hidden[i], units, live_rows)
        sums = jnp.concatenate(
            [jnp.sum(product[:, :128] * head, axis=0, keepdims=True),
             jnp.sum(product[:, 128:] * tail, axis=0, keepdims=True)], axis=1,
        )
        total = jnp.where(row == i, sums, total)
    out[...] = total


def by_slot(table, which, slots):
    live_rows = table.shape[1]
    row = iota((slots, live_rows), 0)
    out = jnp.zeros((slots, live_rows), jnp.float32)
    for k in range(slots):
        out = jnp.where(row == k, table[k * 8 + which:k * 8 + which + 1, :], out)
    return out


def swap_rows(values, m):
    n = values.shape[0]
    row = iota(values.shape, 0)
    out = jnp.zeros_like(values)
    for k in range(n):
        out = jnp.where(row == k, values[k ^ m:(k ^ m) + 1, :], out)
    return out


def grad_kernel(pieces, n_refs, shards, offsets, slots_each, seglen, place, *rest):
    hidden, rest = rest[:shards], rest[shards:]
    refs, rest = rest[:n_refs], rest[n_refs:]
    sums, rest = rest[:len(offsets)], rest[len(offsets):]
    table, ratio_out, grad_out, held, turned, scaled, result, sems, out_sems = rest
    dp, mp = place[0], place[1]
    wide, live_rows = held.shape[3], held.shape[2]
    units = turned.shape[0]
    copies = fetch(pieces, refs, held, sems)
    scale = SCALE / math.sqrt(4 * wide)
    for k in range(shards):
        head, tail = unpack_hidden(hidden[k], units, live_rows)
        turned[:, k * live_rows:(k + 1) * live_rows] = jnp.concatenate([head, tail], axis=1).astype(jnp.bfloat16)

    total = jnp.zeros((shards, live_rows), jnp.float32)
    for ref, m in zip(sums, offsets):
        total = total + swap_rows(ref[...], m)
    logit = by_slot(table, GAP, shards) + total * scale
    adv, dest = by_slot(table, ADV, shards), by_slot(table, DEST, shards)
    counts = jnp.zeros((shards, live_rows), jnp.float32)
    for shard in range(shards):
        here = dest == float(shard)
        tally = jnp.sum(jnp.sum(jnp.where(here, 1.0, 0.0), axis=1, keepdims=True), axis=0, keepdims=True)
        counts = jnp.where(here, tally, counts)
    ratio = jnp.exp(logit)
    squash = jnp.tanh((ratio - 1.0) / 0.2)
    clipped = 1.0 + 0.2 * squash
    slope = jnp.where(ratio * adv <= clipped * adv, 1.0, 1.0 - squash * squash)
    coef = -512.0 * by_slot(table, STALE, shards) * adv * ratio * slope / counts * scale

    mine = jnp.where(dest == dp.astype(jnp.float32), logit, 0.0)
    rank, pos = by_slot(table, RANK, shards), by_slot(table, POS, shards)
    lane = iota((seglen, live_rows), 0).astype(jnp.float32)
    slot = iota((slots_each, live_rows), 0).astype(jnp.float32)
    to_me = dest == dp.astype(jnp.float32)
    for k in range(shards):
        left = jnp.where((slot == rank[k:k + 1]) & to_me[k:k + 1], mine[k:k + 1], 0.0)
        right = jnp.where(lane == pos[k:k + 1], 1.0, 0.0)
        ratio_out[pl.ds(pl.multiple_of((dp ^ k) * slots_each, 8), slots_each)] = lax.dot_general(
            left, right, (((1,), (1,)), ((), ())), precision=EXACT, preferred_element_type=jnp.float32
        )

    eye = iota((live_rows, live_rows), 0) == iota((live_rows, live_rows), 1)
    columns = [jnp.sum(jnp.where(eye, coef[k:k + 1], 0.0), axis=1, keepdims=True) for k in range(shards)]
    writes = []
    for e in range(4):
        for k in range(shards):
            copies[k, e].wait()
            scaled[k * live_rows:(k + 1) * live_rows] = (columns[k] * held[e, k].astype(jnp.float32)).astype(jnp.bfloat16)
        result[e] = jnp.dot(turned[...], scaled[...], preferred_element_type=jnp.float32)
        write = pltpu.make_async_copy(
            result.at[e], grad_out.at[:, pl.ds(pl.multiple_of((mp ^ e) * wide, 128), wide)], out_sems.at[e]
        )
        write.start()
        writes.append(write)
    for write in writes:
        write.wait()


def cube_body(hidden_act, readout, log_gap, advantage, version, lengths, routes, weight):
    shards, quarters = lax.axis_size("dp"), lax.axis_size("mp")
    respond, seglen = log_gap.shape
    live_rows = 7 * respond * seglen // 8
    width = readout.shape[1]
    wide = width // quarters
    units = weight.shape[0]
    rows = packed_rows(units, live_rows)
    slots_each = 2 * respond // shards
    place = jnp.stack([lax.axis_index("dp"), lax.axis_index("mp")]).astype(jnp.int32)
    bf16, f32 = jnp.bfloat16, jnp.float32
    big = pltpu.CompilerParams(vmem_limit_bytes=56 * 1024 * 1024)

    table, sel, own, first, both = pl.pallas_call(
        functools.partial(pack_readout, live_rows, seglen),
        out_shape=(
            jax.ShapeDtypeStruct((8, live_rows), f32),
            jax.ShapeDtypeStruct((live_rows, respond * seglen), bf16),
            jax.ShapeDtypeStruct((quarters, live_rows, wide), bf16),
            jax.ShapeDtypeStruct((live_rows, wide), bf16),
            jax.ShapeDtypeStruct((2 * live_rows, wide), bf16),
        ),
        in_specs=[SMEM] + [VMEM] * 6,
        out_specs=(VMEM,) * 5,
        compiler_params=big,
        name="pack_readout",
    )(place, lengths, routes, log_gap, advantage.reshape(1, respond), version.reshape(1, respond), readout)
    hidden = pl.pallas_call(
        pack_hidden,
        out_shape=(jax.ShapeDtypeStruct((rows, 128), bf16),) * shards,
        in_specs=[SMEM, VMEM, VMEM],
        out_specs=(VMEM,) * shards,
        scratch_shapes=[pltpu.VMEM((shards * rows, 128), bf16)],
        compiler_params=big,
        name="pack_hidden",
    )(place, hidden_act, sel)

    def over_dp(x, m):
        return lax.ppermute(x, "dp", [(s, s ^ m) for s in range(shards)])

    def over_mp(x, m):
        return lax.ppermute(x, "mp", [(s, s ^ m) for s in range(quarters)])

    def over_both(x, m, h):
        pairs = [(s * quarters + t, (s ^ m) * quarters + (t ^ h)) for s in range(shards) for t in range(quarters)]
        return lax.ppermute(x, ("dp", "mp"), pairs)

    def after(x, *others):
        return lax.optimization_barrier((x, *others))[0]

    near = over_dp(first, 2)
    far = over_dp(first, 6)
    beside = over_dp(both, 1)
    arrived = {0: hidden[0]}
    arrived[4] = over_dp(after(hidden[4], near), 4)
    near_far = jnp.concatenate([near, far], axis=0)
    next_far = over_dp(far, 2)
    x_near_far = over_mp(near_far, 2)
    y_near_far = over_dp(near_far, 1)
    arrived[5] = over_dp(after(hidden[5], x_near_far), 5)
    y_next = over_dp(next_far, 1)
    x_next = over_mp(next_far, 2)
    arrived[1] = over_dp(after(hidden[1], next_far), 1)
    arrived[6] = over_dp(after(hidden[6], y_near_far), 6)
    arrived[3] = over_dp(after(hidden[3], y_near_far), 3)
    arrived[7] = over_dp(after(hidden[7], x_near_far), 7)
    xy_near_far = over_mp(y_near_far, 2)
    xy_next = over_mp(y_next, 2)
    arrived[2] = over_dp(after(hidden[2], x_near_far), 2)
    got = [
        (beside, (1, 1), (0, 2)),
        (near_far, (2, 6), (0, 0)),
        (next_far, (4,), (0,)),
        (y_near_far, (3, 7), (0, 0)),
        (y_next, (5,), (0,)),
        (x_near_far, (2, 6), (2, 2)),
        (x_next, (4,), (2,)),
        (xy_near_far, (3, 7), (2, 2)),
        (xy_next, (5,), (2,)),
    ]
    refs = [own]
    pieces = {(0, e): (0, e) for e in range(quarters)}
    for array, ks, es in got:
        for core in (0, 1):
            refs.append(over_mp(array, 1) if core else array)
            for block, (k, e) in enumerate(zip(ks, es)):
                pieces[k, e ^ core] = (len(refs) - 1, block)

    tables = table
    for m in (1, 2, 4):
        tables = jnp.concatenate([tables, over_dp(tables, m)], axis=0)

    hidden_list = [arrived[k] for k in range(shards)]
    sums = pl.pallas_call(
        functools.partial(shift_kernel, pieces, len(refs), tuple(range(shards))),
        out_shape=jax.ShapeDtypeStruct((8, live_rows), f32),
        in_specs=[SMEM, VMEM] + [VMEM] * shards + [ANY] * len(refs),
        out_specs=VMEM,
        scratch_shapes=[
            pltpu.VMEM((quarters, shards, live_rows, wide), bf16),
            pltpu.SemaphoreType.DMA((shards, quarters)),
        ],
        compiler_params=big,
        name="shift_sums",
    )(place, weight, *hidden_list, *refs)

    sums = sums + over_mp(sums, 1)
    sums = sums + over_mp(sums, 2)
    offsets = tuple(range(shards))
    parts = [sums] + [over_dp(sums, m) for m in offsets[1:]]

    log_ratio, weight_grad = pl.pallas_call(
        functools.partial(grad_kernel, pieces, len(refs), shards, offsets, slots_each, seglen),
        out_shape=(
            jax.ShapeDtypeStruct((shards * slots_each, seglen), f32),
            jax.ShapeDtypeStruct((units, width), f32),
        ),
        in_specs=[SMEM] + [VMEM] * shards + [ANY] * len(refs) + [VMEM] * (len(offsets) + 1),
        out_specs=(VMEM, ANY),
        scratch_shapes=[
            pltpu.VMEM((quarters, shards, live_rows, wide), bf16),
            pltpu.VMEM((units, shards * live_rows), bf16),
            pltpu.VMEM((shards * live_rows, wide), bf16),
            pltpu.VMEM((quarters, units, wide), f32),
            pltpu.SemaphoreType.DMA((shards, quarters)),
            pltpu.SemaphoreType.DMA((quarters,)),
        ],
        compiler_params=big,
        name="weight_grad",
    )(place, *hidden_list, *refs, *parts, tables)
    return (log_ratio, weight_grad)


def general_body(hidden_act, readout, log_gap, advantage, version, lengths, routes, weight):
    shards = lax.axis_size("dp")
    respond, seglen = log_gap.shape
    tokens = respond * seglen
    live_rows = 7 * tokens // 8
    width = readout.shape[1]
    units = weight.shape[0]
    slots = 2 * respond // shards
    scale = SCALE / math.sqrt(width)
    f32 = jnp.float32
    dest = routes[:, 0]
    onehot = (dest[:, None] == jnp.arange(shards, dtype=jnp.int32)[None, :]).astype(jnp.int32)
    rank = jnp.sum((jnp.cumsum(onehot, axis=0) - onehot) * onehot, axis=1)
    lens = lengths[0]
    live = (jnp.arange(seglen, dtype=jnp.int32)[None, :] < lens[:, None]).reshape(-1)
    order = jnp.cumsum(live.astype(jnp.int32)) - 1
    select = live[None, :] & (order[None, :] == jnp.arange(live_rows, dtype=jnp.int32)[:, None])
    hidden = jnp.dot(select.astype(jnp.bfloat16), hidden_act)
    hidden = lax.all_to_all(
        hidden.reshape(live_rows, shards, units).swapaxes(0, 1), "dp", split_axis=0, concat_axis=0
    )
    read = lax.all_gather(jnp.dot(select.astype(jnp.bfloat16), readout), "dp", axis=0)

    def one_sum(k, sums):
        product = lax.dot_general(read[k], weight, (((1,), (1,)), ((), ())), preferred_element_type=f32)
        return sums.at[k].set(jnp.sum(product * hidden[k].astype(f32), axis=1))

    sums = lax.fori_loop(0, shards, one_sum, jnp.zeros((shards, live_rows), f32))
    sums = lax.psum(lax.psum_scatter(sums, "dp", scatter_dimension=0, tiled=True)[0], "mp")
    shift = jnp.dot(sums[None, :], select.astype(f32), precision=EXACT).reshape(respond, seglen) * scale
    logit = log_gap + shift
    live = live.reshape(respond, seglen)
    onehot_float = onehot.astype(f32)
    shard_count = lax.psum(jnp.sum(onehot_float * lens.astype(f32)[:, None], axis=0), "dp")
    count_each = jnp.sum(onehot_float * shard_count[None, :], axis=1)
    stale = jnp.power(jnp.float32(0.7), (NVER - 1 - version).astype(f32))
    send = jnp.arange(shards * slots, dtype=jnp.int32)[:, None] == (dest * slots + rank)[None, :]
    log_ratio = lax.all_to_all(
        jnp.dot(send.astype(f32), jnp.where(live, logit, 0.0), precision=EXACT),
        "dp", split_axis=0, concat_axis=0, tiled=True,
    )
    ratio = jnp.exp(logit)
    squash = jnp.tanh((ratio - 1.0) / 0.2)
    clipped = 1.0 + 0.2 * squash
    adv = advantage[:, None]
    slope = jnp.where(ratio * adv <= clipped * adv, 1.0, 1.0 - squash * squash)
    coef = jnp.where(live, -512.0 * stale[:, None] * adv * ratio * slope / count_each[:, None], 0.0)
    coef = jnp.dot(select.astype(f32), coef.reshape(-1, 1), precision=EXACT)[:, 0]
    coefs = lax.all_gather(coef, "dp", axis=0)

    def one_term(k, grad):
        out_grad = (coefs[k][:, None] * scale * read[k].astype(f32)).astype(jnp.bfloat16)
        return grad + lax.dot_general(
            hidden[k], out_grad, (((0,), (0,)), ((), ())), preferred_element_type=f32
        )

    return (log_ratio, lax.fori_loop(0, shards, one_term, jnp.zeros((units, width), f32)))


def body(*args):
    if lax.axis_size("dp") == 8 and lax.axis_size("mp") == 4:
        return cube_body(*args)
    return general_body(*args)


def solution(mesh):
    placed = (
        P("dp", "mp"),
        P("dp", None),
        P("dp", None),
        P("dp"),
        P("dp"),
        P("dp", None),
        P("dp", None),
        P(("mp", "dp"), None),
    )
    return jax.shard_map(
        body,
        mesh=mesh,
        in_specs=placed,
        out_specs=(P("dp", None), P(("mp", "dp"), None)),
        check_vma=False,
    )
```

```python
import functools
import math

import jax
import jax.numpy as jnp
import numpy as np
from jax import lax
from jax.experimental import pallas as pl
from jax.experimental.pallas import tpu as pltpu
from jax.sharding import PartitionSpec as P

NVER = 4
SCALE = 0.15
EXACT = lax.Precision.HIGHEST
VMEM = pl.BlockSpec(memory_space=pltpu.VMEM)
SMEM = pl.BlockSpec(memory_space=pltpu.SMEM)
ANY = pl.BlockSpec(memory_space=pl.ANY)
GAP, ADV, STALE, DEST, RANK, POS = range(6)


def iota(shape, axis):
    return lax.broadcasted_iota(jnp.int32, shape, axis)


def rows_of(*rows):
    n = rows[0].shape[1]
    row = iota((8, n), 0)
    table = jnp.zeros((8, n), jnp.float32)
    for i, values in enumerate(rows):
        table = jnp.where(row == i, values, table)
    return table


def my_place():
    return lax.axis_index("dp"), lax.axis_index("mp")


def live_tokens(live_rows, seglen, lens):
    respond = lens.shape[1]
    tokens = respond * seglen
    expand = (iota((respond, tokens), 0) == lax.div(iota((respond, tokens), 1), seglen)).astype(jnp.bfloat16)
    lens_wide = jnp.broadcast_to(lens.astype(jnp.float32), (16, respond)).astype(jnp.bfloat16)
    by_token = jnp.dot(lens_wide, expand, preferred_element_type=jnp.float32)
    live = lax.rem(iota((16, tokens), 1), seglen).astype(jnp.float32) < by_token
    before = (iota((tokens, tokens), 0) < iota((tokens, tokens), 1)).astype(jnp.bfloat16)
    order = jnp.dot(live.astype(jnp.float32).astype(jnp.bfloat16), before, preferred_element_type=jnp.float32)
    place = jnp.where(live, order, -1.0)[0:1, :]
    return place == iota((live_rows, tokens), 0).astype(jnp.float32)


def pack_first(live_rows, seglen, lens, read, first, both, held, sems):
    _, mp = my_place()
    wide = held.shape[2]
    copies = []
    for i, e in enumerate((0, 2)):
        columns = pl.ds(pl.multiple_of((mp ^ e) * wide, 128), wide)
        copies.append(pltpu.make_async_copy(read.at[:, columns], held.at[i], sems.at[i]))
        copies[-1].start()
    select = live_tokens(live_rows, seglen, lens[...]).astype(jnp.float32).astype(jnp.bfloat16)
    for i in range(2):
        copies[i].wait()
        part = jnp.dot(select, held[i], preferred_element_type=jnp.float32).astype(jnp.bfloat16)
        both[i * live_rows:(i + 1) * live_rows] = part
        if i == 0:
            first[...] = part


def packed_rows(units, live_rows):
    return units * live_rows // 128


def fold_of(live_rows):
    tail = live_rows - 128
    return tail, 128 // math.gcd(tail, 128)


def pack_rest(live_rows, seglen, lens, routes, gap, adv, version, read, hidden, *rest):
    table, own, outs, held = rest[0], rest[1], rest[2:-1], rest[-1]
    dp, mp = my_place()
    seg, respond = gap.shape
    tokens = respond * seg
    chosen = live_tokens(live_rows, seglen, lens[...])
    chosen_f32 = chosen.astype(jnp.float32)
    select = chosen_f32.astype(jnp.bfloat16)
    units = hidden.shape[1] // len(outs)
    tail, fold = fold_of(live_rows)
    short = units // fold
    pieces = tail * fold // 128
    rows = packed_rows(units, live_rows)
    for block in range(0, len(outs), 2):
        turned = lax.dot_general(
            hidden[:, block * units:(block + 2) * units], select, (((0,), (1,)), ((), ())),
            preferred_element_type=jnp.float32,
        )
        for i in range(2):
            part = turned[i * units:(i + 1) * units]
            at = (block + i) * rows
            held[at:at + units] = part[:, :128].astype(jnp.bfloat16)
            wide = jnp.concatenate([part[j * short:(j + 1) * short, 128:] for j in range(fold)], axis=1)
            for j in range(pieces):
                start = at + units + j * short
                held[start:start + short] = wide[:, j * 128:(j + 1) * 128].astype(jnp.bfloat16)
    for k, out in enumerate(outs):
        out[...] = held[pl.ds(pl.multiple_of((dp ^ k) * rows, 16), rows)]

    wide = read.shape[1] // own.shape[0]
    for quarter in range(own.shape[0]):
        own[mp ^ quarter] = jnp.dot(
            select, read[:, quarter * wide:(quarter + 1) * wide], preferred_element_type=jnp.float32
        ).astype(jnp.bfloat16)

    expand = (iota((respond, tokens), 0) == lax.div(iota((respond, tokens), 1), seg)).astype(jnp.float32)
    eye = iota((respond, respond), 0) == iota((respond, respond), 1)
    dest_row = routes[...].astype(jnp.float32)
    dest_col = jnp.sum(jnp.where(eye, dest_row, 0.0), axis=1, keepdims=True)
    earlier = (dest_col == dest_row) & (iota((respond, respond), 0) < iota((respond, respond), 1))
    rank_row = jnp.sum(jnp.where(earlier, 1.0, 0.0), axis=0, keepdims=True)
    age = NVER - 1 - version[...]
    stale = jnp.ones(age.shape, jnp.float32)
    for years in range(1, NVER):
        stale = jnp.where(age == years, jnp.float32(np.float32(0.7) ** years), stale)
    by_token = jnp.dot(
        jnp.concatenate([rows_of(adv[...], stale, dest_row, rank_row), gap[...]], axis=0),
        expand, precision=EXACT, preferred_element_type=jnp.float32,
    )
    pos = lax.rem(iota((seg, tokens), 1), seg)
    gap_row = jnp.sum(jnp.where(pos == iota((seg, tokens), 0), by_token[8:], 0.0), axis=0, keepdims=True)
    table[...] = lax.dot_general(
        rows_of(gap_row, *(by_token[i:i + 1] for i in range(4)), pos[0:1].astype(jnp.float32)),
        chosen_f32, (((1,), (1,)), ((), ())), precision=EXACT, preferred_element_type=jnp.float32,
    )


def unpack_hidden(packed, units, live_rows):
    tail, fold = fold_of(live_rows)
    short = units // fold
    pieces = tail * fold // 128
    wide = jnp.concatenate(
        [packed[units + j * short:units + (j + 1) * short].astype(jnp.float32) for j in range(pieces)], axis=1
    )
    folded = jnp.concatenate([wide[:, j * tail:(j + 1) * tail] for j in range(fold)], axis=0)
    return packed[:units], folded.astype(jnp.bfloat16)


def fetch(pieces, refs, held, sems, slots):
    copies = {}
    live_rows = held.shape[1] // len(slots)
    for e in range(held.shape[0]):
        for i, k in enumerate(slots):
            ref, at = pieces[k, e]
            source = refs[ref].at[at] if ref == 0 else refs[ref].at[pl.ds(at * live_rows, live_rows)]
            copies[k, e] = pltpu.make_async_copy(source, held.at[e, pl.ds(i * live_rows, live_rows)], sems.at[i, e])
            copies[k, e].start()
    return copies


def shift_kernel(pieces, n_refs, slots, live_rows, weight, *rest):
    n = len(slots)
    hidden, refs, rest = rest[:n], rest[n:n + n_refs], rest[n + n_refs:]
    before, (sums, turned, held, rows_held, packed, sems, more_sems) = rest[:-7], rest[-7:]
    _, mp = my_place()
    quarters, wide = held.shape[0], held.shape[2]
    units = weight.shape[0]
    rows_copies = []
    for e in range(quarters):
        columns = pl.ds(pl.multiple_of((mp ^ e) * wide, 128), wide)
        rows_copies.append(pltpu.make_async_copy(weight.at[:, columns], rows_held.at[e], more_sems.at[e]))
        rows_copies[e].start()
    copies = fetch(pieces, refs, held, sems, slots)
    packed_copies = []
    for i in range(n):
        packed_copies.append(pltpu.make_async_copy(hidden[i], packed.at[i], more_sems.at[quarters + i]))
        packed_copies[i].start()
    product = jnp.zeros((units, n * live_rows), jnp.float32)
    for e in range(quarters):
        rows_copies[e].wait()
        for k in slots:
            copies[k, e].wait()
        product += lax.dot_general(
            rows_held[e], held[e], (((1,), (1,)), ((), ())), preferred_element_type=jnp.float32
        )
        if e == 1:
            for i in range(n):
                packed_copies[i].wait()
                head, tail = unpack_hidden(packed[i], units, live_rows)
                turned[:, i * live_rows:(i + 1) * live_rows] = jnp.concatenate([head, tail], axis=1)
    line = jnp.sum(product * turned[...].astype(jnp.float32), axis=0, keepdims=True)
    total = before[0][...] if before else jnp.zeros(sums.shape, jnp.float32)
    row = iota(total.shape, 0)
    for i, k in enumerate(slots):
        total = jnp.where(row == k, line[:, i * live_rows:(i + 1) * live_rows], total)
    sums[...] = total


def by_slot(notes, which):
    slots = 2 * len(notes)
    out = jnp.zeros((slots, notes[0].shape[1]), jnp.float32)
    row = iota(out.shape, 0)
    for k in range(slots):
        at = slots + 8 * (k % 2) + which
        out = jnp.where(row == k, notes[k // 2][at:at + 1, :], out)
    return out


def swap_rows(values, m):
    row = iota(values.shape, 0)
    out = jnp.zeros_like(values)
    for k in range(values.shape[0]):
        out = jnp.where(row == k, values[k ^ m:(k ^ m) + 1, :], out)
    return out


def grad_kernel(pieces, n_refs, groups, slots_each, seglen, *rest):
    order = sum(groups, ())
    shards = len(order)
    hidden, rest = rest[:len(groups)], rest[len(groups):]
    refs, rest = rest[:n_refs], rest[n_refs:]
    notes, rest = rest[:shards // 2], rest[shards // 2:]
    ratio_out, grad_out, held, turned, scaled, result, sems, out_sems = rest
    dp, mp = my_place()
    quarters, wide = held.shape[0], held.shape[2]
    live_rows = notes[0].shape[1]
    copies = fetch(pieces, refs, held, sems, order)
    scale = SCALE / math.sqrt(quarters * wide)
    at = 0
    for part in hidden:
        turned[:, at:at + part.shape[1]] = part[...]
        at += part.shape[1]

    total = notes[0][:shards]
    for i in range(1, len(notes)):
        total = total + swap_rows(notes[i][:shards], 2 * i)
    logit = by_slot(notes, GAP) + total * scale
    adv, dest = by_slot(notes, ADV), by_slot(notes, DEST)
    counts = jnp.zeros((shards, live_rows), jnp.float32)
    for shard in range(shards):
        here = dest == float(shard)
        tally = jnp.sum(jnp.sum(jnp.where(here, 1.0, 0.0), axis=1, keepdims=True), axis=0, keepdims=True)
        counts = jnp.where(here, tally, counts)
    ratio = jnp.exp(logit)
    squash = jnp.tanh((ratio - 1.0) / 0.2)
    clipped = 1.0 + 0.2 * squash
    slope = jnp.where(ratio * adv <= clipped * adv, 1.0, 1.0 - squash * squash)
    coef = -512.0 * by_slot(notes, STALE) * adv * ratio * slope / counts * scale

    eye = iota((live_rows, live_rows), 0) == iota((live_rows, live_rows), 1)
    columns = [jnp.sum(jnp.where(eye, coef[k:k + 1], 0.0), axis=1, keepdims=True) for k in order]
    writes = []
    for e in range(quarters):
        for i, k in enumerate(order):
            copies[k, e].wait()
            rows = slice(i * live_rows, (i + 1) * live_rows)
            scaled[rows] = (columns[i] * held[e, rows].astype(jnp.float32)).astype(jnp.bfloat16)
        result[e] = jnp.dot(turned[...], scaled[...], preferred_element_type=jnp.float32)
        write = pltpu.make_async_copy(
            result.at[e], grad_out.at[:, pl.ds(pl.multiple_of((mp ^ e) * wide, 128), wide)], out_sems.at[e]
        )
        write.start()
        writes.append(write)

    rank, pos = by_slot(notes, RANK), by_slot(notes, POS)
    spots = shards * slots_each
    spot = iota((spots, live_rows), 0).astype(jnp.float32)
    lane = iota((seglen, live_rows), 0).astype(jnp.float32)
    ratios = jnp.zeros((3 * seglen, spots), jnp.float32)
    for k in range(shards):
        to_me = dest[k:k + 1] == dp.astype(jnp.float32)
        target = ((dp ^ k) * slots_each).astype(jnp.float32) + rank[k:k + 1]
        left, spare = [], logit[k:k + 1]
        for _ in range(3):
            part = spare.astype(jnp.bfloat16).astype(jnp.float32)
            left.append(jnp.where(lane == pos[k:k + 1], part, 0.0))
            spare = spare - part
        ratios += lax.dot_general(
            jnp.concatenate(left, axis=0).astype(jnp.bfloat16),
            jnp.where((spot == target) & to_me, 1.0, 0.0).astype(jnp.bfloat16),
            (((1,), (1,)), ((), ())), preferred_element_type=jnp.float32,
        )
    ratio_out[...] = ratios[:seglen] + (ratios[seglen:2 * seglen] + ratios[2 * seglen:])
    for write in writes:
        write.wait()


MOVES = {
    "near": ("first", "dp", 2), "far": ("first", "dp", 6), "next": ("first", "dp", 4), "beside": ("both", "dp", 1),
    "x_n3": ("n3", "mp", 2), "y_n3": ("n3", "dp", 1), "xy_n3": ("y_n3", "mp", 2),
}
MOVES.update({f"h{k}": (f"pack{k}", "dp", k) for k in range(1, 8)})
HOLDS = {
    "beside": ((1, 0), (1, 2)), "n3": ((2, 0), (6, 0), (4, 0)), "y_n3": ((3, 0), (7, 0), (5, 0)),
    "x_n3": ((2, 2), (6, 2), (4, 2)), "xy_n3": ((3, 2), (7, 2), (5, 2)),
}
MOVES.update({"c_" + name: (name, "mp", 1) for name in HOLDS})
PLAN = (
    ("far", "next", "near", "beside", "rest", "h1",),
    ("x_n3", "y_n3", "h4", "h6", "c_beside", "c_n3",),
    ("xy_n3", "h7", "h5", "h3", "h2", "c_x_n3", "c_y_n3", "early",),
    ("c_xy_n3",),
)
BESIDES = {"early": ("h7",), "c_xy_n3": ("early",)}
EARLY = (0, 1, 2, 6, 4, )
LATE = (3, 7, 5, )


def cube_body(hidden_act, readout, log_gap, advantage, version, lengths, routes, weight):
    shards, quarters = lax.axis_size("dp"), lax.axis_size("mp")
    respond, seglen = log_gap.shape
    live_rows = 7 * respond * seglen // 8
    width = readout.shape[1]
    wide = width // quarters
    units = weight.shape[0]
    rows = packed_rows(units, live_rows)
    slots_each = 2 * respond // shards
    bf16, f32 = jnp.bfloat16, jnp.float32
    big = pltpu.CompilerParams(vmem_limit_bytes=56 * 1024 * 1024)

    def cost(flops, moved):
        return pl.CostEstimate(flops=int(flops), bytes_accessed=int(moved), transcendentals=0)

    def over_dp(x, m):
        return lax.ppermute(x, "dp", [(s, s ^ m) for s in range(shards)])

    def over_mp(x, m):
        return lax.ppermute(x, "mp", [(s, s ^ m) for s in range(quarters)])

    def over_both(x, m, h):
        pairs = [(s * quarters + t, (s ^ m) * quarters + (t ^ h)) for s in range(shards) for t in range(quarters)]
        return lax.ppermute(x, ("dp", "mp"), pairs)

    got = {}

    def after(x, names):
        names = [name for name in names if name in got]
        return lax.optimization_barrier((x, *(got[name] for name in names)))[0] if names else x

    got["first"], got["both"] = pl.pallas_call(
        functools.partial(pack_first, live_rows, seglen),
        out_shape=(jax.ShapeDtypeStruct((live_rows, wide), bf16), jax.ShapeDtypeStruct((2 * live_rows, wide), bf16)),
        in_specs=[VMEM, ANY],
        out_specs=(VMEM, VMEM),
        scratch_shapes=[pltpu.VMEM((2, respond * seglen, wide), bf16), pltpu.SemaphoreType.DMA((2,))],
        compiler_params=big,
        name="pack_first",
    )(lengths, readout)

    def rest(gates):
        table, own, *hidden = pl.pallas_call(
            functools.partial(pack_rest, live_rows, seglen),
            out_shape=(
                jax.ShapeDtypeStruct((8, live_rows), f32),
                jax.ShapeDtypeStruct((quarters, live_rows, wide), bf16),
            ) + (jax.ShapeDtypeStruct((rows, 128), bf16),) * shards,
            in_specs=[VMEM] * 7,
            out_specs=(VMEM,) * (shards + 2),
            scratch_shapes=[pltpu.VMEM((shards * rows, 128), bf16)],
            compiler_params=big,
            cost_estimate=cost(2e9, 8e6),
            name="pack_rest",
        )(after(lengths, gates), routes.reshape(1, respond), log_gap.T, advantage.reshape(1, respond),
          version.reshape(1, respond), readout, hidden_act)
        got.update({"table": table, "own": own, "h0": hidden[0], "rest": table})
        got.update({f"pack{k}": hidden[k] for k in range(1, shards)})

    def used(slots):
        names, places = ["own"], {(0, e): (0, e) for e in range(quarters)}
        for name, blocks in HOLDS.items():
            for core in (0, 1):
                if any(k in slots for k, _ in blocks):
                    for block, (k, e) in enumerate(blocks):
                        places[k, e ^ core] = (len(names), block)
                    names.append("c_" + name if core else name)
        return [got[name] for name in names], places

    groups = (EARLY, LATE) if EARLY else (LATE,)
    turned = []

    def shift_sums(slots, *before, gates=()):
        refs, places = used(slots)
        refs[0] = after(refs[0], gates)
        sums, part = pl.pallas_call(
            functools.partial(shift_kernel, places, len(refs), slots, live_rows),
            out_shape=(
                jax.ShapeDtypeStruct((shards, live_rows), f32),
                jax.ShapeDtypeStruct((units, len(slots) * live_rows), bf16),
            ),
            in_specs=[ANY] * (1 + len(slots) + len(refs)) + [VMEM] * len(before),
            out_specs=(VMEM, VMEM),
            scratch_shapes=[
                pltpu.VMEM((quarters, len(slots) * live_rows, wide), bf16),
                pltpu.VMEM((quarters, units, wide), bf16),
                pltpu.VMEM((len(slots), rows, 128), bf16),
                pltpu.SemaphoreType.DMA((len(slots), quarters)),
                pltpu.SemaphoreType.DMA((quarters + len(slots),)),
            ],
            compiler_params=big,
            cost_estimate=cost(2 * units * len(slots) * live_rows * width, 2 * len(slots) * live_rows * width),
            name="shift_sums",
        )(weight, *(got[f"h{k}"] for k in slots), *refs, *before)
        turned.append(part)
        return sums

    gates = ()
    for steps in PLAN:
        moved = []
        for step in steps:
            if step == "rest":
                rest(gates)
                moved.append(step)
            elif step == "early":
                got[step] = shift_sums(EARLY, gates=BESIDES.get(step, ()))
            else:
                source, axis, m = MOVES[step]
                if source == "n3" and source not in got:
                    got[source] = jnp.concatenate([got["near"], got["far"], got["next"]], axis=0)
                core = [name for name in moved if name[:2] == "c_" and step[:2] == "c_"]
                got[step] = (over_dp if axis == "dp" else over_mp)(
                    after(got[source], (*gates, *core, *BESIDES.get(step, ()))), m
                )
                moved.append(step)
        gates = tuple(moved)
    sums = shift_sums(LATE, *([got["early"]] if EARLY else []))

    sums = sums + over_mp(sums, 1)
    table = got["table"]
    beside = over_dp(jnp.concatenate([sums, table], axis=0), 1)
    across = beside[:shards] + over_both(sums, 1, 2)
    sums = sums + over_mp(sums, 2)
    note = jnp.concatenate(
        [sums + jnp.concatenate([across[k ^ 1:(k ^ 1) + 1] for k in range(shards)], axis=0), table, beside[shards:]], axis=0
    )
    notes = [note] + [over_dp(note, m) for m in (2, 4, 6)]

    order = sum(groups, ())
    refs, places = used(order)
    log_ratio, weight_grad = pl.pallas_call(
        functools.partial(grad_kernel, places, len(refs), groups, slots_each, seglen),
        out_shape=(
            jax.ShapeDtypeStruct((seglen, shards * slots_each), f32),
            jax.ShapeDtypeStruct((units, width), f32),
        ),
        in_specs=[VMEM] * len(groups) + [ANY] * len(refs) + [VMEM] * len(notes),
        out_specs=(VMEM, ANY),
        scratch_shapes=[
            pltpu.VMEM((quarters, shards * live_rows, wide), bf16),
            pltpu.VMEM((units, shards * live_rows), bf16),
            pltpu.VMEM((shards * live_rows, wide), bf16),
            pltpu.VMEM((quarters, units, wide), f32),
            pltpu.SemaphoreType.DMA((shards, quarters)),
            pltpu.SemaphoreType.DMA((quarters,)),
        ],
        compiler_params=big,
        cost_estimate=cost(2 * units * shards * live_rows * width, 2 * shards * live_rows * width + 4 * units * width),
        name="weight_grad",
    )(*turned, *refs, *notes)
    return (log_ratio.T, weight_grad)


def general_body(hidden_act, readout, log_gap, advantage, version, lengths, routes, weight):
    shards = lax.axis_size("dp")
    respond, seglen = log_gap.shape
    tokens = respond * seglen
    live_rows = 7 * tokens // 8
    width = readout.shape[1]
    units = weight.shape[0]
    slots = 2 * respond // shards
    scale = SCALE / math.sqrt(width)
    f32 = jnp.float32
    dest = routes[:, 0]
    onehot = (dest[:, None] == jnp.arange(shards, dtype=jnp.int32)[None, :]).astype(jnp.int32)
    rank = jnp.sum((jnp.cumsum(onehot, axis=0) - onehot) * onehot, axis=1)
    lens = lengths[0]
    live = (jnp.arange(seglen, dtype=jnp.int32)[None, :] < lens[:, None]).reshape(-1)
    order = jnp.cumsum(live.astype(jnp.int32)) - 1
    select = live[None, :] & (order[None, :] == jnp.arange(live_rows, dtype=jnp.int32)[:, None])
    hidden = jnp.dot(select.astype(jnp.bfloat16), hidden_act)
    hidden = lax.all_to_all(
        hidden.reshape(live_rows, shards, units).swapaxes(0, 1), "dp", split_axis=0, concat_axis=0
    )
    read = lax.all_gather(jnp.dot(select.astype(jnp.bfloat16), readout), "dp", axis=0)

    def one_sum(k, sums):
        product = lax.dot_general(read[k], weight, (((1,), (1,)), ((), ())), preferred_element_type=f32)
        return sums.at[k].set(jnp.sum(product * hidden[k].astype(f32), axis=1))

    sums = lax.fori_loop(0, shards, one_sum, jnp.zeros((shards, live_rows), f32))
    sums = lax.psum(lax.psum_scatter(sums, "dp", scatter_dimension=0, tiled=True)[0], "mp")
    shift = jnp.dot(sums[None, :], select.astype(f32), precision=EXACT).reshape(respond, seglen) * scale
    logit = log_gap + shift
    live = live.reshape(respond, seglen)
    onehot_float = onehot.astype(f32)
    shard_count = lax.psum(jnp.sum(onehot_float * lens.astype(f32)[:, None], axis=0), "dp")
    count_each = jnp.sum(onehot_float * shard_count[None, :], axis=1)
    stale = jnp.power(jnp.float32(0.7), (NVER - 1 - version).astype(f32))
    send = jnp.arange(shards * slots, dtype=jnp.int32)[:, None] == (dest * slots + rank)[None, :]
    log_ratio = lax.all_to_all(
        jnp.dot(send.astype(f32), jnp.where(live, logit, 0.0), precision=EXACT),
        "dp", split_axis=0, concat_axis=0, tiled=True,
    )
    ratio = jnp.exp(logit)
    squash = jnp.tanh((ratio - 1.0) / 0.2)
    clipped = 1.0 + 0.2 * squash
    adv = advantage[:, None]
    slope = jnp.where(ratio * adv <= clipped * adv, 1.0, 1.0 - squash * squash)
    coef = jnp.where(live, -512.0 * stale[:, None] * adv * ratio * slope / count_each[:, None], 0.0)
    coef = jnp.dot(select.astype(f32), coef.reshape(-1, 1), precision=EXACT)[:, 0]
    coefs = lax.all_gather(coef, "dp", axis=0)

    def one_term(k, grad):
        out_grad = (coefs[k][:, None] * scale * read[k].astype(f32)).astype(jnp.bfloat16)
        return grad + lax.dot_general(
            hidden[k], out_grad, (((0,), (0,)), ((), ())), preferred_element_type=f32
        )

    return (log_ratio, lax.fori_loop(0, shards, one_term, jnp.zeros((units, width), f32)))


def body(*args):
    if lax.axis_size("dp") == 8 and lax.axis_size("mp") == 4:
        return cube_body(*args)
    return general_body(*args)


def solution(mesh):
    placed = (
        P("dp", "mp"),
        P("dp", None),
        P("dp", None),
        P("dp"),
        P("dp"),
        P("dp", None),
        P("dp", None),
        P(("mp", "dp"), None),
    )
    return jax.shard_map(
        body,
        mesh=mesh,
        in_specs=placed,
        out_specs=(P("dp", None), P(("mp", "dp"), None)),
        check_vma=False,
    )
```

```python
import functools
import math

import jax
import jax.numpy as jnp
import numpy as np
from jax import lax
from jax.experimental import pallas as pl
from jax.experimental.pallas import tpu as pltpu
from jax.sharding import PartitionSpec as P

NVER = 4
SCALE = 0.15
EXACT = lax.Precision.HIGHEST
VMEM = pl.BlockSpec(memory_space=pltpu.VMEM)
SMEM = pl.BlockSpec(memory_space=pltpu.SMEM)
ANY = pl.BlockSpec(memory_space=pl.ANY)
GAP, ADV, STALE, DEST, RANK, POS = range(6)


def iota(shape, axis):
    return lax.broadcasted_iota(jnp.int32, shape, axis)


def rows_of(*rows):
    n = rows[0].shape[1]
    row = iota((8, n), 0)
    table = jnp.zeros((8, n), jnp.float32)
    for i, values in enumerate(rows):
        table = jnp.where(row == i, values, table)
    return table


def my_place():
    return lax.axis_index("dp"), lax.axis_index("mp")


def live_tokens(live_rows, seglen, lens):
    respond = lens.shape[1]
    tokens = respond * seglen
    expand = (iota((respond, tokens), 0) == lax.div(iota((respond, tokens), 1), seglen)).astype(jnp.bfloat16)
    lens_wide = jnp.broadcast_to(lens.astype(jnp.float32), (16, respond)).astype(jnp.bfloat16)
    by_token = jnp.dot(lens_wide, expand, preferred_element_type=jnp.float32)
    live = lax.rem(iota((16, tokens), 1), seglen).astype(jnp.float32) < by_token
    before = (iota((tokens, tokens), 0) < iota((tokens, tokens), 1)).astype(jnp.bfloat16)
    order = jnp.dot(live.astype(jnp.float32).astype(jnp.bfloat16), before, preferred_element_type=jnp.float32)
    place = jnp.where(live, order, -1.0)[0:1, :]
    return place == iota((live_rows, tokens), 0).astype(jnp.float32)


def pack_first(live_rows, seglen, lens, read, first, both, held, sems):
    _, mp = my_place()
    wide = held.shape[2]
    copies = []
    for i, e in enumerate((0, 2)):
        columns = pl.ds(pl.multiple_of((mp ^ e) * wide, 128), wide)
        copies.append(pltpu.make_async_copy(read.at[:, columns], held.at[i], sems.at[i]))
        copies[-1].start()
    select = live_tokens(live_rows, seglen, lens[...]).astype(jnp.float32).astype(jnp.bfloat16)
    for i in range(2):
        copies[i].wait()
        part = jnp.dot(select, held[i], preferred_element_type=jnp.float32).astype(jnp.bfloat16)
        both[i * live_rows:(i + 1) * live_rows] = part
        if i == 0:
            first[...] = part


def packed_rows(units, live_rows):
    return units * live_rows // 128


def fold_of(live_rows):
    tail = live_rows - 128
    return tail, 128 // math.gcd(tail, 128)


def pack_rest(live_rows, seglen, lens, routes, gap, adv, version, read, hidden, *rest):
    table, own, outs, held = rest[0], rest[1], rest[2:-1], rest[-1]
    dp, mp = my_place()
    seg, respond = gap.shape
    tokens = respond * seg
    chosen = live_tokens(live_rows, seglen, lens[...])
    chosen_f32 = chosen.astype(jnp.float32)
    select = chosen_f32.astype(jnp.bfloat16)
    units = hidden.shape[1] // len(outs)
    tail, fold = fold_of(live_rows)
    short = units // fold
    pieces = tail * fold // 128
    rows = packed_rows(units, live_rows)
    for block in range(0, len(outs), 2):
        turned = lax.dot_general(
            hidden[:, block * units:(block + 2) * units], select, (((0,), (1,)), ((), ())),
            preferred_element_type=jnp.float32,
        )
        for i in range(2):
            part = turned[i * units:(i + 1) * units]
            at = (block + i) * rows
            held[at:at + units] = part[:, :128].astype(jnp.bfloat16)
            wide = jnp.concatenate([part[j * short:(j + 1) * short, 128:] for j in range(fold)], axis=1)
            for j in range(pieces):
                start = at + units + j * short
                held[start:start + short] = wide[:, j * 128:(j + 1) * 128].astype(jnp.bfloat16)
    for k, out in enumerate(outs):
        out[...] = held[pl.ds(pl.multiple_of((dp ^ k) * rows, 16), rows)]

    wide = read.shape[1] // own.shape[0]
    for quarter in range(own.shape[0]):
        own[mp ^ quarter] = jnp.dot(
            select, read[:, quarter * wide:(quarter + 1) * wide], preferred_element_type=jnp.float32
        ).astype(jnp.bfloat16)

    expand = (iota((respond, tokens), 0) == lax.div(iota((respond, tokens), 1), seg)).astype(jnp.float32)
    eye = iota((respond, respond), 0) == iota((respond, respond), 1)
    dest_row = routes[...].astype(jnp.float32)
    dest_col = jnp.sum(jnp.where(eye, dest_row, 0.0), axis=1, keepdims=True)
    earlier = (dest_col == dest_row) & (iota((respond, respond), 0) < iota((respond, respond), 1))
    rank_row = jnp.sum(jnp.where(earlier, 1.0, 0.0), axis=0, keepdims=True)
    age = NVER - 1 - version[...]
    stale = jnp.ones(age.shape, jnp.float32)
    for years in range(1, NVER):
        stale = jnp.where(age == years, jnp.float32(np.float32(0.7) ** years), stale)
    by_token = jnp.dot(
        jnp.concatenate([rows_of(adv[...], stale, dest_row, rank_row), gap[...]], axis=0),
        expand, precision=EXACT, preferred_element_type=jnp.float32,
    )
    pos = lax.rem(iota((seg, tokens), 1), seg)
    gap_row = jnp.sum(jnp.where(pos == iota((seg, tokens), 0), by_token[8:], 0.0), axis=0, keepdims=True)
    table[...] = lax.dot_general(
        rows_of(gap_row, *(by_token[i:i + 1] for i in range(4)), pos[0:1].astype(jnp.float32)),
        chosen_f32, (((1,), (1,)), ((), ())), precision=EXACT, preferred_element_type=jnp.float32,
    )


def unpack_hidden(packed, units, live_rows):
    tail, fold = fold_of(live_rows)
    short = units // fold
    pieces = tail * fold // 128
    wide = jnp.concatenate(
        [packed[units + j * short:units + (j + 1) * short].astype(jnp.float32) for j in range(pieces)], axis=1
    )
    folded = jnp.concatenate([wide[:, j * tail:(j + 1) * tail] for j in range(fold)], axis=0)
    return packed[:units], folded.astype(jnp.bfloat16)


def fetch(pieces, refs, held, sems, slots):
    copies = {}
    quarters = sems.shape[1]
    live_rows, wide = held.shape[0] // len(slots), held.shape[1] // quarters
    for e in range(quarters):
        for i, k in enumerate(slots):
            ref, at = pieces[k, e]
            source = refs[ref].at[at] if ref == 0 else refs[ref].at[pl.ds(at * live_rows, live_rows)]
            target = held.at[pl.ds(i * live_rows, live_rows), pl.ds(e * wide, wide)]
            copies[k, e] = pltpu.make_async_copy(source, target, sems.at[i, e])
            copies[k, e].start()
    return copies


def shift_kernel(pieces, n_refs, slots, live_rows, weight, *rest):
    n = len(slots)
    hidden, refs, rest = rest[:n], rest[n:n + n_refs], rest[n + n_refs:]
    before, (sums, turned, held, rows_held, packed, sems, more_sems) = rest[:-7], rest[-7:]
    _, mp = my_place()
    quarters = sems.shape[1]
    units, width = weight.shape
    wide = width // quarters
    packed_copies, rows_copies = [], []
    for i in range(n):
        packed_copies.append(pltpu.make_async_copy(hidden[i], packed.at[i], more_sems.at[quarters + i]))
        packed_copies[i].start()
    for e in range(quarters):
        columns = pl.ds(pl.multiple_of((mp ^ e) * wide, 128), wide)
        rows_copies.append(
            pltpu.make_async_copy(weight.at[:, columns], rows_held.at[:, pl.ds(e * wide, wide)], more_sems.at[e])
        )
        rows_copies[e].start()
    copies = fetch(pieces, refs, held, sems, slots)
    for i in range(n):
        packed_copies[i].wait()
        head, tail = unpack_hidden(packed[i], units, live_rows)
        turned[:, i * live_rows:(i + 1) * live_rows] = jnp.concatenate([head, tail], axis=1)
    for e in range(quarters):
        rows_copies[e].wait()
        for k in slots:
            copies[k, e].wait()
    product = lax.dot_general(
        rows_held[...], held[...], (((1,), (1,)), ((), ())), preferred_element_type=jnp.float32
    )
    line = jnp.sum(product * turned[...].astype(jnp.float32), axis=0, keepdims=True)
    total = before[0][...] if before else jnp.zeros(sums.shape, jnp.float32)
    row = iota(total.shape, 0)
    for i, k in enumerate(slots):
        total = jnp.where(row == k, line[:, i * live_rows:(i + 1) * live_rows], total)
    sums[...] = total


def by_slot(notes, which):
    slots = 2 * len(notes)
    out = jnp.zeros((slots, notes[0].shape[1]), jnp.float32)
    row = iota(out.shape, 0)
    for k in range(slots):
        at = slots + 8 * (k % 2) + which
        out = jnp.where(row == k, notes[k // 2][at:at + 1, :], out)
    return out


def swap_rows(values, m):
    row = iota(values.shape, 0)
    out = jnp.zeros_like(values)
    for k in range(values.shape[0]):
        out = jnp.where(row == k, values[k ^ m:(k ^ m) + 1, :], out)
    return out


def grad_kernel(pieces, n_refs, groups, slots_each, seglen, *rest):
    order = sum(groups, ())
    shards = len(order)
    hidden, rest = rest[:len(groups)], rest[len(groups):]
    refs, rest = rest[:n_refs], rest[n_refs:]
    notes, rest = rest[:shards // 2], rest[shards // 2:]
    ratio_out, grad_out, held, turned, scaled, result, sems, out_sems = rest
    dp, mp = my_place()
    quarters, wide = sems.shape[1], held.shape[1] // sems.shape[1]
    live_rows = notes[0].shape[1]
    copies = fetch(pieces, refs, held, sems, order)
    scale = SCALE / math.sqrt(quarters * wide)
    at = 0
    for part in hidden:
        turned[:, at:at + part.shape[1]] = part[...]
        at += part.shape[1]

    total = notes[0][:shards]
    for i in range(1, len(notes)):
        total = total + swap_rows(notes[i][:shards], 2 * i)
    logit = by_slot(notes, GAP) + total * scale
    adv, dest = by_slot(notes, ADV), by_slot(notes, DEST)
    counts = jnp.zeros((shards, live_rows), jnp.float32)
    for shard in range(shards):
        here = dest == float(shard)
        tally = jnp.sum(jnp.sum(jnp.where(here, 1.0, 0.0), axis=1, keepdims=True), axis=0, keepdims=True)
        counts = jnp.where(here, tally, counts)
    ratio = jnp.exp(logit)
    squash = jnp.tanh((ratio - 1.0) / 0.2)
    clipped = 1.0 + 0.2 * squash
    slope = jnp.where(ratio * adv <= clipped * adv, 1.0, 1.0 - squash * squash)
    coef = -512.0 * by_slot(notes, STALE) * adv * ratio * slope / counts * scale

    eye = iota((live_rows, live_rows), 0) == iota((live_rows, live_rows), 1)
    columns = [jnp.sum(jnp.where(eye, coef[k:k + 1], 0.0), axis=1, keepdims=True) for k in order]

    def scale_rows(e):
        for k in order:
            copies[k, e].wait()
        for i in range(shards):
            rows = slice(i * live_rows, (i + 1) * live_rows)
            part = held[rows, e * wide:(e + 1) * wide].astype(jnp.float32)
            scaled[e % 2, rows] = (columns[i] * part).astype(jnp.bfloat16)

    writes = []
    scale_rows(0)
    for e in range(quarters):
        if e + 1 < quarters:
            scale_rows(e + 1)
        result[e] = jnp.dot(turned[...], scaled[e % 2], preferred_element_type=jnp.float32)
        write = pltpu.make_async_copy(
            result.at[e], grad_out.at[:, pl.ds(pl.multiple_of((mp ^ e) * wide, 128), wide)], out_sems.at[e]
        )
        write.start()
        writes.append(write)

    rank, pos = by_slot(notes, RANK), by_slot(notes, POS)
    spots = shards * slots_each
    spot = iota((spots, live_rows), 0).astype(jnp.float32)
    lane = iota((seglen, live_rows), 0).astype(jnp.float32)
    ratios = jnp.zeros((3 * seglen, spots), jnp.float32)
    for k in range(shards):
        to_me = dest[k:k + 1] == dp.astype(jnp.float32)
        target = ((dp ^ k) * slots_each).astype(jnp.float32) + rank[k:k + 1]
        left, spare = [], logit[k:k + 1]
        for _ in range(3):
            part = spare.astype(jnp.bfloat16).astype(jnp.float32)
            left.append(jnp.where(lane == pos[k:k + 1], part, 0.0))
            spare = spare - part
        ratios += lax.dot_general(
            jnp.concatenate(left, axis=0).astype(jnp.bfloat16),
            jnp.where((spot == target) & to_me, 1.0, 0.0).astype(jnp.bfloat16),
            (((1,), (1,)), ((), ())), preferred_element_type=jnp.float32,
        )
    ratio_out[...] = ratios[:seglen] + (ratios[seglen:2 * seglen] + ratios[2 * seglen:])
    for write in writes:
        write.wait()


MOVES = {
    "near": ("first", "dp", 2), "far": ("first", "dp", 6), "next": ("first", "dp", 4), "beside": ("both", "dp", 1),
    "x_n3": ("n3", "mp", 2), "y_n3": ("n3", "dp", 1), "xy_n3": ("y_n3", "mp", 2),
}
MOVES.update({f"h{k}": (f"pack{k}", "dp", k) for k in range(1, 8)})
HOLDS = {
    "beside": ((1, 0), (1, 2)), "n3": ((2, 0), (6, 0), (4, 0)), "y_n3": ((3, 0), (7, 0), (5, 0)),
    "x_n3": ((2, 2), (6, 2), (4, 2)), "xy_n3": ((3, 2), (7, 2), (5, 2)),
}
MOVES.update({"c_" + name: (name, "mp", 1) for name in HOLDS})
PLAN = (
    ("far", "next", "near", "beside", "rest", "h1",),
    ("x_n3", "y_n3", "h4", "h6", "c_beside", "c_n3",),
    ("xy_n3", "h7", "h5", "h3", "h2", "c_x_n3", "c_y_n3", "early",),
    ("c_xy_n3",),
)
BESIDES = {"early": ("h7",), "c_xy_n3": ("early",)}
EARLY = (0, 1, 2, 6, 4, )
LATE = (3, 7, 5, )


def cube_body(hidden_act, readout, log_gap, advantage, version, lengths, routes, weight):
    shards, quarters = lax.axis_size("dp"), lax.axis_size("mp")
    respond, seglen = log_gap.shape
    live_rows = 7 * respond * seglen // 8
    width = readout.shape[1]
    wide = width // quarters
    units = weight.shape[0]
    rows = packed_rows(units, live_rows)
    slots_each = 2 * respond // shards
    bf16, f32 = jnp.bfloat16, jnp.float32
    def room(mib):
        return pltpu.CompilerParams(vmem_limit_bytes=mib * 1024 * 1024)

    def cost(flops, moved):
        return pl.CostEstimate(flops=int(flops), bytes_accessed=int(moved), transcendentals=0)

    def over_dp(x, m):
        return lax.ppermute(x, "dp", [(s, s ^ m) for s in range(shards)])

    def over_mp(x, m):
        return lax.ppermute(x, "mp", [(s, s ^ m) for s in range(quarters)])

    def over_both(x, m, h):
        pairs = [(s * quarters + t, (s ^ m) * quarters + (t ^ h)) for s in range(shards) for t in range(quarters)]
        return lax.ppermute(x, ("dp", "mp"), pairs)

    got = {}

    def after(x, names):
        names = [name for name in names if name in got]
        return lax.optimization_barrier((x, *(got[name] for name in names)))[0] if names else x

    got["first"], got["both"] = pl.pallas_call(
        functools.partial(pack_first, live_rows, seglen),
        out_shape=(jax.ShapeDtypeStruct((live_rows, wide), bf16), jax.ShapeDtypeStruct((2 * live_rows, wide), bf16)),
        in_specs=[VMEM, ANY],
        out_specs=(VMEM, VMEM),
        scratch_shapes=[pltpu.VMEM((2, respond * seglen, wide), bf16), pltpu.SemaphoreType.DMA((2,))],
        compiler_params=room(12),
        name="pack_first",
    )(lengths, readout)

    def rest(gates):
        table, own, *hidden = pl.pallas_call(
            functools.partial(pack_rest, live_rows, seglen),
            out_shape=(
                jax.ShapeDtypeStruct((8, live_rows), f32),
                jax.ShapeDtypeStruct((quarters, live_rows, wide), bf16),
            ) + (jax.ShapeDtypeStruct((rows, 128), bf16),) * shards,
            in_specs=[VMEM] * 7,
            out_specs=(VMEM,) * (shards + 2),
            scratch_shapes=[pltpu.VMEM((shards * rows, 128), bf16)],
            compiler_params=room(20),
            cost_estimate=cost(2e9, 8e6),
            name="pack_rest",
        )(after(lengths, gates), routes.reshape(1, respond), log_gap.T, advantage.reshape(1, respond),
          version.reshape(1, respond), readout, hidden_act)
        got.update({"table": table, "own": own, "h0": hidden[0], "rest": table})
        got.update({f"pack{k}": hidden[k] for k in range(1, shards)})

    def used(slots):
        names, places = ["own"], {(0, e): (0, e) for e in range(quarters)}
        for name, blocks in HOLDS.items():
            for core in (0, 1):
                if any(k in slots for k, _ in blocks):
                    for block, (k, e) in enumerate(blocks):
                        places[k, e ^ core] = (len(names), block)
                    names.append("c_" + name if core else name)
        return [got[name] for name in names], places

    groups = (EARLY, LATE) if EARLY else (LATE,)
    turned = []

    def shift_sums(slots, *before, gates=()):
        refs, places = used(slots)
        refs[0] = after(refs[0], gates)
        sums, part = pl.pallas_call(
            functools.partial(shift_kernel, places, len(refs), slots, live_rows),
            out_shape=(
                jax.ShapeDtypeStruct((shards, live_rows), f32),
                jax.ShapeDtypeStruct((units, len(slots) * live_rows), bf16),
            ),
            in_specs=[ANY] * (1 + len(slots) + len(refs)) + [VMEM] * len(before),
            out_specs=(VMEM, VMEM),
            scratch_shapes=[
                pltpu.VMEM((len(slots) * live_rows, width), bf16),
                pltpu.VMEM((units, width), bf16),
                pltpu.VMEM((len(slots), rows, 128), bf16),
                pltpu.SemaphoreType.DMA((len(slots), quarters)),
                pltpu.SemaphoreType.DMA((quarters + len(slots),)),
            ],
            compiler_params=room(20),
            cost_estimate=cost(2 * units * len(slots) * live_rows * width, 2 * len(slots) * live_rows * width),
            name="shift_sums",
        )(weight, *(got[f"h{k}"] for k in slots), *refs, *before)
        turned.append(part)
        return sums

    gates = ()
    for steps in PLAN:
        moved = []
        for step in steps:
            if step == "rest":
                rest(gates)
                moved.append(step)
            elif step == "early":
                got[step] = shift_sums(EARLY, gates=BESIDES.get(step, ()))
            else:
                source, axis, m = MOVES[step]
                if source == "n3" and source not in got:
                    got[source] = jnp.concatenate([got["near"], got["far"], got["next"]], axis=0)
                core = [name for name in moved if name[:2] == "c_" and step[:2] == "c_"]
                got[step] = (over_dp if axis == "dp" else over_mp)(
                    after(got[source], (*gates, *core, *BESIDES.get(step, ()))), m
                )
                moved.append(step)
        gates = tuple(moved)
    sums = shift_sums(LATE, *([got["early"]] if EARLY else []))

    sums = sums + over_mp(sums, 1)
    table = got["table"]
    beside = over_dp(jnp.concatenate([sums, table], axis=0), 1)
    across = beside[:shards] + over_both(sums, 1, 2)
    sums = sums + over_mp(sums, 2)
    note = jnp.concatenate(
        [sums + jnp.concatenate([across[k ^ 1:(k ^ 1) + 1] for k in range(shards)], axis=0), table, beside[shards:]], axis=0
    )
    notes = [note] + [over_dp(note, m) for m in (2, 4, 6)]

    order = sum(groups, ())
    refs, places = used(order)
    log_ratio, weight_grad = pl.pallas_call(
        functools.partial(grad_kernel, places, len(refs), groups, slots_each, seglen),
        out_shape=(
            jax.ShapeDtypeStruct((seglen, shards * slots_each), f32),
            jax.ShapeDtypeStruct((units, width), f32),
        ),
        in_specs=[VMEM] * len(groups) + [ANY] * len(refs) + [VMEM] * len(notes),
        out_specs=(VMEM, ANY),
        scratch_shapes=[
            pltpu.VMEM((shards * live_rows, width), bf16),
            pltpu.VMEM((units, shards * live_rows), bf16),
            pltpu.VMEM((2, shards * live_rows, wide), bf16),
            pltpu.VMEM((quarters, units, wide), f32),
            pltpu.SemaphoreType.DMA((shards, quarters)),
            pltpu.SemaphoreType.DMA((quarters,)),
        ],
        compiler_params=room(56),
        cost_estimate=cost(2 * units * shards * live_rows * width, 2 * shards * live_rows * width + 4 * units * width),
        name="weight_grad",
    )(*turned, *refs, *notes)
    return (log_ratio.T, weight_grad)


def general_body(hidden_act, readout, log_gap, advantage, version, lengths, routes, weight):
    shards = lax.axis_size("dp")
    respond, seglen = log_gap.shape
    tokens = respond * seglen
    live_rows = 7 * tokens // 8
    width = readout.shape[1]
    units = weight.shape[0]
    slots = 2 * respond // shards
    scale = SCALE / math.sqrt(width)
    f32 = jnp.float32
    dest = routes[:, 0]
    onehot = (dest[:, None] == jnp.arange(shards, dtype=jnp.int32)[None, :]).astype(jnp.int32)
    rank = jnp.sum((jnp.cumsum(onehot, axis=0) - onehot) * onehot, axis=1)
    lens = lengths[0]
    live = (jnp.arange(seglen, dtype=jnp.int32)[None, :] < lens[:, None]).reshape(-1)
    order = jnp.cumsum(live.astype(jnp.int32)) - 1
    select = live[None, :] & (order[None, :] == jnp.arange(live_rows, dtype=jnp.int32)[:, None])
    hidden = jnp.dot(select.astype(jnp.bfloat16), hidden_act)
    hidden = lax.all_to_all(
        hidden.reshape(live_rows, shards, units).swapaxes(0, 1), "dp", split_axis=0, concat_axis=0
    )
    read = lax.all_gather(jnp.dot(select.astype(jnp.bfloat16), readout), "dp", axis=0)

    def one_sum(k, sums):
        product = lax.dot_general(read[k], weight, (((1,), (1,)), ((), ())), preferred_element_type=f32)
        return sums.at[k].set(jnp.sum(product * hidden[k].astype(f32), axis=1))

    sums = lax.fori_loop(0, shards, one_sum, jnp.zeros((shards, live_rows), f32))
    sums = lax.psum(lax.psum_scatter(sums, "dp", scatter_dimension=0, tiled=True)[0], "mp")
    shift = jnp.dot(sums[None, :], select.astype(f32), precision=EXACT).reshape(respond, seglen) * scale
    logit = log_gap + shift
    live = live.reshape(respond, seglen)
    onehot_float = onehot.astype(f32)
    shard_count = lax.psum(jnp.sum(onehot_float * lens.astype(f32)[:, None], axis=0), "dp")
    count_each = jnp.sum(onehot_float * shard_count[None, :], axis=1)
    stale = jnp.power(jnp.float32(0.7), (NVER - 1 - version).astype(f32))
    send = jnp.arange(shards * slots, dtype=jnp.int32)[:, None] == (dest * slots + rank)[None, :]
    log_ratio = lax.all_to_all(
        jnp.dot(send.astype(f32), jnp.where(live, logit, 0.0), precision=EXACT),
        "dp", split_axis=0, concat_axis=0, tiled=True,
    )
    ratio = jnp.exp(logit)
    squash = jnp.tanh((ratio - 1.0) / 0.2)
    clipped = 1.0 + 0.2 * squash
    adv = advantage[:, None]
    slope = jnp.where(ratio * adv <= clipped * adv, 1.0, 1.0 - squash * squash)
    coef = jnp.where(live, -512.0 * stale[:, None] * adv * ratio * slope / count_each[:, None], 0.0)
    coef = jnp.dot(select.astype(f32), coef.reshape(-1, 1), precision=EXACT)[:, 0]
    coefs = lax.all_gather(coef, "dp", axis=0)

    def one_term(k, grad):
        out_grad = (coefs[k][:, None] * scale * read[k].astype(f32)).astype(jnp.bfloat16)
        return grad + lax.dot_general(
            hidden[k], out_grad, (((0,), (0,)), ((), ())), preferred_element_type=f32
        )

    return (log_ratio, lax.fori_loop(0, shards, one_term, jnp.zeros((units, width), f32)))


def body(*args):
    if lax.axis_size("dp") == 8 and lax.axis_size("mp") == 4:
        return cube_body(*args)
    return general_body(*args)


def solution(mesh):
    placed = (
        P("dp", "mp"),
        P("dp", None),
        P("dp", None),
        P("dp"),
        P("dp"),
        P("dp", None),
        P("dp", None),
        P(("mp", "dp"), None),
    )
    return jax.shard_map(
        body,
        mesh=mesh,
        in_specs=placed,
        out_specs=(P("dp", None), P(("mp", "dp"), None)),
        check_vma=False,
    )
```

```python
import functools
import math

import jax
import jax.numpy as jnp
import numpy as np
from jax import lax
from jax.experimental import pallas as pl
from jax.experimental.pallas import tpu as pltpu
from jax.sharding import PartitionSpec as P

NVER = 4
SCALE = 0.15
EXACT = lax.Precision.HIGHEST
VMEM = pl.BlockSpec(memory_space=pltpu.VMEM)
SMEM = pl.BlockSpec(memory_space=pltpu.SMEM)
ANY = pl.BlockSpec(memory_space=pl.ANY)
GAP, ADV, STALE, DEST, RANK, POS = range(6)


def iota(shape, axis):
    return lax.broadcasted_iota(jnp.int32, shape, axis)


def rows_of(*rows):
    n = rows[0].shape[1]
    row = iota((8, n), 0)
    table = jnp.zeros((8, n), jnp.float32)
    for i, values in enumerate(rows):
        table = jnp.where(row == i, values, table)
    return table


def my_place():
    return lax.axis_index("dp"), lax.axis_index("mp")


def live_tokens(live_rows, seglen, lens):
    respond = lens.shape[1]
    tokens = respond * seglen
    expand = (iota((respond, tokens), 0) == lax.div(iota((respond, tokens), 1), seglen)).astype(jnp.bfloat16)
    lens_wide = jnp.broadcast_to(lens.astype(jnp.float32), (16, respond)).astype(jnp.bfloat16)
    by_token = jnp.dot(lens_wide, expand, preferred_element_type=jnp.float32)
    live = lax.rem(iota((16, tokens), 1), seglen).astype(jnp.float32) < by_token
    before = (iota((tokens, tokens), 0) < iota((tokens, tokens), 1)).astype(jnp.bfloat16)
    order = jnp.dot(live.astype(jnp.float32).astype(jnp.bfloat16), before, preferred_element_type=jnp.float32)
    place = jnp.where(live, order, -1.0)[0:1, :]
    return place == iota((live_rows, tokens), 0).astype(jnp.float32)


def pack_first(live_rows, seglen, lens, read, first, both, held, sems):
    _, mp = my_place()
    wide = held.shape[2]
    copies = []
    for i, e in enumerate((0, 2)):
        columns = pl.ds(pl.multiple_of((mp ^ e) * wide, 128), wide)
        copies.append(pltpu.make_async_copy(read.at[:, columns], held.at[i], sems.at[i]))
        copies[-1].start()
    select = live_tokens(live_rows, seglen, lens[...]).astype(jnp.float32).astype(jnp.bfloat16)
    for i in range(2):
        copies[i].wait()
        part = jnp.dot(select, held[i], preferred_element_type=jnp.float32).astype(jnp.bfloat16)
        both[i * live_rows:(i + 1) * live_rows] = part
        if i == 0:
            first[...] = part


def packed_rows(units, live_rows):
    return units * live_rows // 128


def fold_of(live_rows):
    tail = live_rows - 128
    return tail, 128 // math.gcd(tail, 128)


def pack_rest(live_rows, seglen, lens, routes, gap, adv, version, read, hidden, *rest):
    table, own, outs, held = rest[0], rest[1], rest[2:-1], rest[-1]
    dp, mp = my_place()
    seg, respond = gap.shape
    tokens = respond * seg
    chosen = live_tokens(live_rows, seglen, lens[...])
    chosen_f32 = chosen.astype(jnp.float32)
    select = chosen_f32.astype(jnp.bfloat16)
    units = hidden.shape[1] // len(outs)
    tail, fold = fold_of(live_rows)
    short = units // fold
    pieces = tail * fold // 128
    rows = packed_rows(units, live_rows)
    for block in range(0, len(outs), 2):
        turned = lax.dot_general(
            hidden[:, block * units:(block + 2) * units], select, (((0,), (1,)), ((), ())),
            preferred_element_type=jnp.float32,
        )
        for i in range(2):
            part = turned[i * units:(i + 1) * units]
            at = (block + i) * rows
            held[at:at + units] = part[:, :128].astype(jnp.bfloat16)
            wide = jnp.concatenate([part[j * short:(j + 1) * short, 128:] for j in range(fold)], axis=1)
            for j in range(pieces):
                start = at + units + j * short
                held[start:start + short] = wide[:, j * 128:(j + 1) * 128].astype(jnp.bfloat16)
    for k, out in enumerate(outs):
        out[...] = held[pl.ds(pl.multiple_of((dp ^ k) * rows, 16), rows)]

    wide = read.shape[1] // own.shape[0]
    for quarter in range(own.shape[0]):
        own[mp ^ quarter] = jnp.dot(
            select, read[:, quarter * wide:(quarter + 1) * wide], preferred_element_type=jnp.float32
        ).astype(jnp.bfloat16)

    expand = (iota((respond, tokens), 0) == lax.div(iota((respond, tokens), 1), seg)).astype(jnp.float32)
    eye = iota((respond, respond), 0) == iota((respond, respond), 1)
    dest_row = routes[...].astype(jnp.float32)
    dest_col = jnp.sum(jnp.where(eye, dest_row, 0.0), axis=1, keepdims=True)
    earlier = (dest_col == dest_row) & (iota((respond, respond), 0) < iota((respond, respond), 1))
    rank_row = jnp.sum(jnp.where(earlier, 1.0, 0.0), axis=0, keepdims=True)
    age = NVER - 1 - version[...]
    stale = jnp.ones(age.shape, jnp.float32)
    for years in range(1, NVER):
        stale = jnp.where(age == years, jnp.float32(np.float32(0.7) ** years), stale)
    by_token = jnp.dot(
        jnp.concatenate([rows_of(adv[...], stale, dest_row, rank_row), gap[...]], axis=0),
        expand, precision=EXACT, preferred_element_type=jnp.float32,
    )
    pos = lax.rem(iota((seg, tokens), 1), seg)
    gap_row = jnp.sum(jnp.where(pos == iota((seg, tokens), 0), by_token[8:], 0.0), axis=0, keepdims=True)
    table[...] = lax.dot_general(
        rows_of(gap_row, *(by_token[i:i + 1] for i in range(4)), pos[0:1].astype(jnp.float32)),
        chosen_f32, (((1,), (1,)), ((), ())), precision=EXACT, preferred_element_type=jnp.float32,
    )


def unpack_hidden(packed, units, live_rows):
    tail, fold = fold_of(live_rows)
    short = units // fold
    pieces = tail * fold // 128
    wide = jnp.concatenate(
        [packed[units + j * short:units + (j + 1) * short].astype(jnp.float32) for j in range(pieces)], axis=1
    )
    folded = jnp.concatenate([wide[:, j * tail:(j + 1) * tail] for j in range(fold)], axis=0)
    return packed[:units], folded.astype(jnp.bfloat16)


def fetch(pieces, refs, held, sems, slots):
    copies = {}
    quarters = sems.shape[1]
    live_rows, wide = held.shape[0] // len(slots), held.shape[1] // quarters
    for e in range(quarters):
        for i, k in enumerate(slots):
            ref, at = pieces[k, e]
            source = refs[ref].at[at] if ref == 0 else refs[ref].at[pl.ds(at * live_rows, live_rows)]
            target = held.at[pl.ds(i * live_rows, live_rows), pl.ds(e * wide, wide)]
            copies[k, e] = pltpu.make_async_copy(source, target, sems.at[i, e])
            copies[k, e].start()
    return copies


def shift_kernel(pieces, n_refs, slots, live_rows, weight, *rest):
    n = len(slots)
    hidden, refs, rest = rest[:n], rest[n:n + n_refs], rest[n + n_refs:]
    before, (sums, turned, held, rows_held, packed, sems, more_sems) = rest[:-7], rest[-7:]
    _, mp = my_place()
    quarters = sems.shape[1]
    units, width = weight.shape
    wide = width // quarters
    packed_copies, rows_copies = [], []
    for i in range(n):
        packed_copies.append(pltpu.make_async_copy(hidden[i], packed.at[i], more_sems.at[quarters + i]))
        packed_copies[i].start()
    for e in range(quarters):
        columns = pl.ds(pl.multiple_of((mp ^ e) * wide, 128), wide)
        rows_copies.append(
            pltpu.make_async_copy(weight.at[:, columns], rows_held.at[:, pl.ds(e * wide, wide)], more_sems.at[e])
        )
        rows_copies[e].start()
    copies = fetch(pieces, refs, held, sems, slots)
    for i in range(n):
        packed_copies[i].wait()
        head, tail = unpack_hidden(packed[i], units, live_rows)
        turned[:, i * live_rows:(i + 1) * live_rows] = jnp.concatenate([head, tail], axis=1)
    for e in range(quarters):
        rows_copies[e].wait()
        for k in slots:
            copies[k, e].wait()
    product = lax.dot_general(
        rows_held[...], held[...], (((1,), (1,)), ((), ())), preferred_element_type=jnp.float32
    )
    line = jnp.sum(product * turned[...].astype(jnp.float32), axis=0, keepdims=True)
    total = before[0][...] if before else jnp.zeros(sums.shape, jnp.float32)
    row = iota(total.shape, 0)
    for i, k in enumerate(slots):
        total = jnp.where(row == k, line[:, i * live_rows:(i + 1) * live_rows], total)
    sums[...] = total


def by_slot(notes, which):
    slots = 2 * len(notes)
    out = jnp.zeros((slots, notes[0].shape[1]), jnp.float32)
    row = iota(out.shape, 0)
    for k in range(slots):
        at = slots + 8 * (k % 2) + which
        out = jnp.where(row == k, notes[k // 2][at:at + 1, :], out)
    return out


def swap_rows(values, m):
    row = iota(values.shape, 0)
    out = jnp.zeros_like(values)
    for k in range(values.shape[0]):
        out = jnp.where(row == k, values[k ^ m:(k ^ m) + 1, :], out)
    return out


def grad_kernel(pieces, n_refs, groups, slots_each, seglen, *rest):
    order = sum(groups, ())
    shards = len(order)
    hidden, rest = rest[:len(groups)], rest[len(groups):]
    refs, late_rows, rest = rest[:n_refs], rest[n_refs], rest[n_refs + 1:]
    notes, rest = rest[:shards // 2], rest[shards // 2:]
    ratio_out, grad_out, held, turned, scaled, result, sems, out_sems = rest
    dp, mp = my_place()
    quarters, wide = sems.shape[1], held.shape[1] // sems.shape[1]
    live_rows = notes[0].shape[1]
    copies = fetch(pieces, refs, held, sems, groups[0])
    scale = SCALE / math.sqrt(quarters * wide)
    at = 0
    for part in hidden:
        turned[:, at:at + part.shape[1]] = part[...]
        at += part.shape[1]

    total = notes[0][:shards]
    for i in range(1, len(notes)):
        total = total + swap_rows(notes[i][:shards], 2 * i)
    logit = by_slot(notes, GAP) + total * scale
    adv, dest = by_slot(notes, ADV), by_slot(notes, DEST)
    counts = jnp.zeros((shards, live_rows), jnp.float32)
    for shard in range(shards):
        here = dest == float(shard)
        tally = jnp.sum(jnp.sum(jnp.where(here, 1.0, 0.0), axis=1, keepdims=True), axis=0, keepdims=True)
        counts = jnp.where(here, tally, counts)
    ratio = jnp.exp(logit)
    squash = jnp.tanh((ratio - 1.0) / 0.2)
    clipped = 1.0 + 0.2 * squash
    slope = jnp.where(ratio * adv <= clipped * adv, 1.0, 1.0 - squash * squash)
    coef = -512.0 * by_slot(notes, STALE) * adv * ratio * slope / counts * scale

    eye = iota((live_rows, live_rows), 0) == iota((live_rows, live_rows), 1)
    columns = [jnp.sum(jnp.where(eye, coef[k:k + 1], 0.0), axis=1, keepdims=True) for k in order]

    def scale_rows(e):
        early = len(groups[0])
        for i in range(shards):
            source, at = (held, i) if i < early else (late_rows, i - early)
            part = source[at * live_rows:(at + 1) * live_rows, e * wide:(e + 1) * wide].astype(jnp.float32)
            scaled[e % 2, i * live_rows:(i + 1) * live_rows] = (columns[i] * part).astype(jnp.bfloat16)

    for copy in copies.values():
        copy.wait()
    writes = []
    scale_rows(0)
    for e in range(quarters):
        if e + 1 < quarters:
            scale_rows(e + 1)
        result[e] = jnp.dot(turned[...], scaled[e % 2], preferred_element_type=jnp.float32)
        write = pltpu.make_async_copy(
            result.at[e], grad_out.at[:, pl.ds(pl.multiple_of((mp ^ e) * wide, 128), wide)], out_sems.at[e]
        )
        write.start()
        writes.append(write)

    rank, pos = by_slot(notes, RANK), by_slot(notes, POS)
    spots = shards * slots_each
    spot = iota((spots, live_rows), 0).astype(jnp.float32)
    lane = iota((seglen, live_rows), 0).astype(jnp.float32)
    ratios = jnp.zeros((3 * seglen, spots), jnp.float32)
    for k in range(shards):
        to_me = dest[k:k + 1] == dp.astype(jnp.float32)
        target = ((dp ^ k) * slots_each).astype(jnp.float32) + rank[k:k + 1]
        left, spare = [], logit[k:k + 1]
        for _ in range(3):
            part = spare.astype(jnp.bfloat16).astype(jnp.float32)
            left.append(jnp.where(lane == pos[k:k + 1], part, 0.0))
            spare = spare - part
        ratios += lax.dot_general(
            jnp.concatenate(left, axis=0).astype(jnp.bfloat16),
            jnp.where((spot == target) & to_me, 1.0, 0.0).astype(jnp.bfloat16),
            (((1,), (1,)), ((), ())), preferred_element_type=jnp.float32,
        )
    ratio_out[...] = ratios[:seglen] + (ratios[seglen:2 * seglen] + ratios[2 * seglen:])
    for write in writes:
        write.wait()


MOVES = {
    "near": ("first", "dp", 2), "far": ("first", "dp", 6), "next": ("first", "dp", 4), "beside": ("both", "dp", 1),
    "x_n3": ("n3", "mp", 2), "y_n3": ("n3", "dp", 1), "xy_n3": ("y_n3", "mp", 2),
}
MOVES.update({f"h{k}": (f"pack{k}", "dp", k) for k in range(1, 8)})
HOLDS = {
    "beside": ((1, 0), (1, 2)), "n3": ((2, 0), (6, 0), (4, 0)), "y_n3": ((3, 0), (7, 0), (5, 0)),
    "x_n3": ((2, 2), (6, 2), (4, 2)), "xy_n3": ((3, 2), (7, 2), (5, 2)),
}
MOVES.update({"c_" + name: (name, "mp", 1) for name in HOLDS})
PLAN = (
    ("far", "next", "near", "beside", "rest", "h1",),
    ("x_n3", "y_n3", "h4", "h6", "c_beside", "c_n3",),
    ("xy_n3", "h7", "h5", "h3", "h2", "c_x_n3", "c_y_n3", "early",),
    ("c_xy_n3",),
)
BESIDES = {"h3": ("c_y_n3",), "early": ("h7",), "c_xy_n3": ("early",)}
FREE = ()
EARLY = (0, 1, 2, 6, 4, )
LATE = (3, 7, 5, )


def cube_body(hidden_act, readout, log_gap, advantage, version, lengths, routes, weight):
    shards, quarters = lax.axis_size("dp"), lax.axis_size("mp")
    respond, seglen = log_gap.shape
    live_rows = 7 * respond * seglen // 8
    width = readout.shape[1]
    wide = width // quarters
    units = weight.shape[0]
    rows = packed_rows(units, live_rows)
    slots_each = 2 * respond // shards
    bf16, f32 = jnp.bfloat16, jnp.float32
    def room(mib):
        return pltpu.CompilerParams(vmem_limit_bytes=mib * 1024 * 1024)

    def cost(flops, moved):
        return pl.CostEstimate(flops=int(flops), bytes_accessed=int(moved), transcendentals=0)

    def over_dp(x, m):
        return lax.ppermute(x, "dp", [(s, s ^ m) for s in range(shards)])

    def over_mp(x, m):
        return lax.ppermute(x, "mp", [(s, s ^ m) for s in range(quarters)])

    def over_both(x, m, h):
        pairs = [(s * quarters + t, (s ^ m) * quarters + (t ^ h)) for s in range(shards) for t in range(quarters)]
        return lax.ppermute(x, ("dp", "mp"), pairs)

    got = {}

    def after(x, names):
        names = [name for name in names if name in got]
        return lax.optimization_barrier((x, *(got[name] for name in names)))[0] if names else x

    got["first"], got["both"] = pl.pallas_call(
        functools.partial(pack_first, live_rows, seglen),
        out_shape=(jax.ShapeDtypeStruct((live_rows, wide), bf16), jax.ShapeDtypeStruct((2 * live_rows, wide), bf16)),
        in_specs=[VMEM, ANY],
        out_specs=(VMEM, VMEM),
        scratch_shapes=[pltpu.VMEM((2, respond * seglen, wide), bf16), pltpu.SemaphoreType.DMA((2,))],
        compiler_params=room(12),
        name="pack_first",
    )(lengths, readout)

    def rest(gates):
        table, own, *hidden = pl.pallas_call(
            functools.partial(pack_rest, live_rows, seglen),
            out_shape=(
                jax.ShapeDtypeStruct((8, live_rows), f32),
                jax.ShapeDtypeStruct((quarters, live_rows, wide), bf16),
            ) + (jax.ShapeDtypeStruct((rows, 128), bf16),) * shards,
            in_specs=[VMEM] * 7,
            out_specs=(VMEM,) * (shards + 2),
            scratch_shapes=[pltpu.VMEM((shards * rows, 128), bf16)],
            compiler_params=room(20),
            cost_estimate=cost(2e9, 8e6),
            name="pack_rest",
        )(after(lengths, gates), routes.reshape(1, respond), log_gap.T, advantage.reshape(1, respond),
          version.reshape(1, respond), readout, hidden_act)
        got.update({"table": table, "own": own, "h0": hidden[0], "rest": table})
        got.update({f"pack{k}": hidden[k] for k in range(1, shards)})

    def used(slots):
        names, places = ["own"], {(0, e): (0, e) for e in range(quarters)}
        for name, blocks in HOLDS.items():
            for core in (0, 1):
                if any(k in slots for k, _ in blocks):
                    for block, (k, e) in enumerate(blocks):
                        places[k, e ^ core] = (len(names), block)
                    names.append("c_" + name if core else name)
        return [got[name] for name in names], places

    groups = (EARLY, LATE)
    turned, late_rows = [], []

    def shift_sums(slots, *before, gates=(), keep=False):
        refs, places = used(slots)
        refs[0] = after(refs[0], gates)
        rows_shape = (len(slots) * live_rows, width)
        sums, part, *kept = pl.pallas_call(
            functools.partial(shift_kernel, places, len(refs), slots, live_rows),
            out_shape=(
                jax.ShapeDtypeStruct((shards, live_rows), f32),
                jax.ShapeDtypeStruct((units, len(slots) * live_rows), bf16),
            ) + (jax.ShapeDtypeStruct(rows_shape, bf16),) * keep,
            in_specs=[ANY] * (1 + len(slots) + len(refs)) + [VMEM] * len(before),
            out_specs=(VMEM,) * (2 + keep),
            scratch_shapes=[pltpu.VMEM(rows_shape, bf16)] * (not keep) + [
                pltpu.VMEM((units, width), bf16),
                pltpu.VMEM((len(slots), rows, 128), bf16),
                pltpu.SemaphoreType.DMA((len(slots), quarters)),
                pltpu.SemaphoreType.DMA((quarters + len(slots),)),
            ],
            compiler_params=room(20),
            cost_estimate=cost(2 * units * len(slots) * live_rows * width, 2 * len(slots) * live_rows * width),
            name="shift_sums",
        )(weight, *(got[f"h{k}"] for k in slots), *refs, *before)
        turned.append(part)
        late_rows.extend(kept)
        return sums

    gates = ()
    for steps in PLAN:
        moved = []
        for step in steps:
            if step == "rest":
                rest(gates)
                moved.append(step)
            elif step == "early":
                got[step] = shift_sums(EARLY, gates=BESIDES.get(step, ()))
            else:
                source, axis, m = MOVES[step]
                if source == "n3" and source not in got:
                    got[source] = jnp.concatenate([got["near"], got["far"], got["next"]], axis=0)
                core = [name for name in moved if name[:2] == "c_" and step[:2] == "c_"]
                got[step] = (over_dp if axis == "dp" else over_mp)(
                    after(got[source], (*gates, *core, *BESIDES.get(step, ()))), m
                )
                if step not in FREE:
                    moved.append(step)
        gates = tuple(moved)
    sums = shift_sums(LATE, got["early"], keep=True)

    sums = sums + over_mp(sums, 1)
    table = got["table"]
    beside = over_dp(jnp.concatenate([sums, table], axis=0), 1)
    across = beside[:shards] + over_both(sums, 1, 2)
    sums = sums + over_mp(sums, 2)
    note = jnp.concatenate(
        [sums + jnp.concatenate([across[k ^ 1:(k ^ 1) + 1] for k in range(shards)], axis=0), table, beside[shards:]], axis=0
    )
    notes = [note] + [over_dp(note, m) for m in (2, 4, 6)]

    refs, places = used(EARLY)
    log_ratio, weight_grad = pl.pallas_call(
        functools.partial(grad_kernel, places, len(refs), groups, slots_each, seglen),
        out_shape=(
            jax.ShapeDtypeStruct((seglen, shards * slots_each), f32),
            jax.ShapeDtypeStruct((units, width), f32),
        ),
        in_specs=[VMEM] * len(groups) + [ANY] * len(refs) + [VMEM] * (1 + len(notes)),
        out_specs=(VMEM, ANY),
        scratch_shapes=[
            pltpu.VMEM((len(EARLY) * live_rows, width), bf16),
            pltpu.VMEM((units, shards * live_rows), bf16),
            pltpu.VMEM((2, shards * live_rows, wide), bf16),
            pltpu.VMEM((quarters, units, wide), f32),
            pltpu.SemaphoreType.DMA((len(EARLY), quarters)),
            pltpu.SemaphoreType.DMA((quarters,)),
        ],
        compiler_params=room(52),
        cost_estimate=cost(2 * units * shards * live_rows * width, 2 * shards * live_rows * width + 4 * units * width),
        name="weight_grad",
    )(*turned, *refs, *late_rows, *notes)
    return (log_ratio.T, weight_grad)


def general_body(hidden_act, readout, log_gap, advantage, version, lengths, routes, weight):
    shards = lax.axis_size("dp")
    respond, seglen = log_gap.shape
    tokens = respond * seglen
    live_rows = 7 * tokens // 8
    width = readout.shape[1]
    units = weight.shape[0]
    slots = 2 * respond // shards
    scale = SCALE / math.sqrt(width)
    f32 = jnp.float32
    dest = routes[:, 0]
    onehot = (dest[:, None] == jnp.arange(shards, dtype=jnp.int32)[None, :]).astype(jnp.int32)
    rank = jnp.sum((jnp.cumsum(onehot, axis=0) - onehot) * onehot, axis=1)
    lens = lengths[0]
    live = (jnp.arange(seglen, dtype=jnp.int32)[None, :] < lens[:, None]).reshape(-1)
    order = jnp.cumsum(live.astype(jnp.int32)) - 1
    select = live[None, :] & (order[None, :] == jnp.arange(live_rows, dtype=jnp.int32)[:, None])
    hidden = jnp.dot(select.astype(jnp.bfloat16), hidden_act)
    hidden = lax.all_to_all(
        hidden.reshape(live_rows, shards, units).swapaxes(0, 1), "dp", split_axis=0, concat_axis=0
    )
    read = lax.all_gather(jnp.dot(select.astype(jnp.bfloat16), readout), "dp", axis=0)

    def one_sum(k, sums):
        product = lax.dot_general(read[k], weight, (((1,), (1,)), ((), ())), preferred_element_type=f32)
        return sums.at[k].set(jnp.sum(product * hidden[k].astype(f32), axis=1))

    sums = lax.fori_loop(0, shards, one_sum, jnp.zeros((shards, live_rows), f32))
    sums = lax.psum(lax.psum_scatter(sums, "dp", scatter_dimension=0, tiled=True)[0], "mp")
    shift = jnp.dot(sums[None, :], select.astype(f32), precision=EXACT).reshape(respond, seglen) * scale
    logit = log_gap + shift
    live = live.reshape(respond, seglen)
    onehot_float = onehot.astype(f32)
    shard_count = lax.psum(jnp.sum(onehot_float * lens.astype(f32)[:, None], axis=0), "dp")
    count_each = jnp.sum(onehot_float * shard_count[None, :], axis=1)
    stale = jnp.power(jnp.float32(0.7), (NVER - 1 - version).astype(f32))
    send = jnp.arange(shards * slots, dtype=jnp.int32)[:, None] == (dest * slots + rank)[None, :]
    log_ratio = lax.all_to_all(
        jnp.dot(send.astype(f32), jnp.where(live, logit, 0.0), precision=EXACT),
        "dp", split_axis=0, concat_axis=0, tiled=True,
    )
    ratio = jnp.exp(logit)
    squash = jnp.tanh((ratio - 1.0) / 0.2)
    clipped = 1.0 + 0.2 * squash
    adv = advantage[:, None]
    slope = jnp.where(ratio * adv <= clipped * adv, 1.0, 1.0 - squash * squash)
    coef = jnp.where(live, -512.0 * stale[:, None] * adv * ratio * slope / count_each[:, None], 0.0)
    coef = jnp.dot(select.astype(f32), coef.reshape(-1, 1), precision=EXACT)[:, 0]
    coefs = lax.all_gather(coef, "dp", axis=0)

    def one_term(k, grad):
        out_grad = (coefs[k][:, None] * scale * read[k].astype(f32)).astype(jnp.bfloat16)
        return grad + lax.dot_general(
            hidden[k], out_grad, (((0,), (0,)), ((), ())), preferred_element_type=f32
        )

    return (log_ratio, lax.fori_loop(0, shards, one_term, jnp.zeros((units, width), f32)))


def body(*args):
    if lax.axis_size("dp") == 8 and lax.axis_size("mp") == 4:
        return cube_body(*args)
    return general_body(*args)


def solution(mesh):
    placed = (
        P("dp", "mp"),
        P("dp", None),
        P("dp", None),
        P("dp"),
        P("dp"),
        P("dp", None),
        P("dp", None),
        P(("mp", "dp"), None),
    )
    return jax.shard_map(
        body,
        mesh=mesh,
        in_specs=placed,
        out_specs=(P("dp", None), P(("mp", "dp"), None)),
        check_vma=False,
    )
```

```python
import functools
import math

import jax
import jax.numpy as jnp
import numpy as np
from jax import lax
from jax.experimental import pallas as pl
from jax.experimental.pallas import tpu as pltpu
from jax.sharding import PartitionSpec as P

NVER = 4
SCALE = 0.15
EXACT = lax.Precision.HIGHEST
VMEM = pl.BlockSpec(memory_space=pltpu.VMEM)
SMEM = pl.BlockSpec(memory_space=pltpu.SMEM)
ANY = pl.BlockSpec(memory_space=pl.ANY)
GAP, ADV, STALE, DEST, RANK, POS = range(6)


def iota(shape, axis):
    return lax.broadcasted_iota(jnp.int32, shape, axis)


def rows_of(*rows):
    n = rows[0].shape[1]
    row = iota((8, n), 0)
    table = jnp.zeros((8, n), jnp.float32)
    for i, values in enumerate(rows):
        table = jnp.where(row == i, values, table)
    return table


def my_place():
    return lax.axis_index("dp"), lax.axis_index("mp")


def live_tokens(live_rows, seglen, lens):
    respond = lens.shape[1]
    tokens = respond * seglen
    expand = (iota((respond, tokens), 0) == lax.div(iota((respond, tokens), 1), seglen)).astype(jnp.bfloat16)
    lens_wide = jnp.broadcast_to(lens.astype(jnp.float32), (16, respond)).astype(jnp.bfloat16)
    by_token = jnp.dot(lens_wide, expand, preferred_element_type=jnp.float32)
    live = lax.rem(iota((16, tokens), 1), seglen).astype(jnp.float32) < by_token
    before = (iota((tokens, tokens), 0) < iota((tokens, tokens), 1)).astype(jnp.bfloat16)
    order = jnp.dot(live.astype(jnp.float32).astype(jnp.bfloat16), before, preferred_element_type=jnp.float32)
    place = jnp.where(live, order, -1.0)[0:1, :]
    return place == iota((live_rows, tokens), 0).astype(jnp.float32)


def pack_first(live_rows, seglen, lens, read, first, both, held, sems):
    _, mp = my_place()
    wide = held.shape[2]
    copies = []
    for i, e in enumerate((0, 2)):
        columns = pl.ds(pl.multiple_of((mp ^ e) * wide, 128), wide)
        copies.append(pltpu.make_async_copy(read.at[:, columns], held.at[i], sems.at[i]))
        copies[-1].start()
    select = live_tokens(live_rows, seglen, lens[...]).astype(jnp.float32).astype(jnp.bfloat16)
    for i in range(2):
        copies[i].wait()
        part = jnp.dot(select, held[i], preferred_element_type=jnp.float32).astype(jnp.bfloat16)
        both[i * live_rows:(i + 1) * live_rows] = part
        if i == 0:
            first[...] = part


def packed_rows(units, live_rows):
    return units * live_rows // 128


def fold_of(live_rows):
    tail = live_rows - 128
    return tail, 128 // math.gcd(tail, 128)


def pack_rest(live_rows, seglen, lens, routes, gap, adv, version, read, hidden, *rest):
    table, own, outs, held = rest[0], rest[1], rest[2:-1], rest[-1]
    dp, mp = my_place()
    seg, respond = gap.shape
    tokens = respond * seg
    chosen = live_tokens(live_rows, seglen, lens[...])
    chosen_f32 = chosen.astype(jnp.float32)
    select = chosen_f32.astype(jnp.bfloat16)
    units = hidden.shape[1] // len(outs)
    tail, fold = fold_of(live_rows)
    short = units // fold
    pieces = tail * fold // 128
    rows = packed_rows(units, live_rows)
    for block in range(0, len(outs), 2):
        turned = lax.dot_general(
            hidden[:, block * units:(block + 2) * units], select, (((0,), (1,)), ((), ())),
            preferred_element_type=jnp.float32,
        )
        for i in range(2):
            part = turned[i * units:(i + 1) * units]
            at = (block + i) * rows
            held[at:at + units] = part[:, :128].astype(jnp.bfloat16)
            wide = jnp.concatenate([part[j * short:(j + 1) * short, 128:] for j in range(fold)], axis=1)
            for j in range(pieces):
                start = at + units + j * short
                held[start:start + short] = wide[:, j * 128:(j + 1) * 128].astype(jnp.bfloat16)
    for k, out in enumerate(outs):
        out[...] = held[pl.ds(pl.multiple_of((dp ^ k) * rows, 16), rows)]

    wide = read.shape[1] // own.shape[0]
    for quarter in range(own.shape[0]):
        own[mp ^ quarter] = jnp.dot(
            select, read[:, quarter * wide:(quarter + 1) * wide], preferred_element_type=jnp.float32
        ).astype(jnp.bfloat16)

    expand = (iota((respond, tokens), 0) == lax.div(iota((respond, tokens), 1), seg)).astype(jnp.float32)
    eye = iota((respond, respond), 0) == iota((respond, respond), 1)
    dest_row = routes[...].astype(jnp.float32)
    dest_col = jnp.sum(jnp.where(eye, dest_row, 0.0), axis=1, keepdims=True)
    earlier = (dest_col == dest_row) & (iota((respond, respond), 0) < iota((respond, respond), 1))
    rank_row = jnp.sum(jnp.where(earlier, 1.0, 0.0), axis=0, keepdims=True)
    age = NVER - 1 - version[...]
    stale = jnp.ones(age.shape, jnp.float32)
    for years in range(1, NVER):
        stale = jnp.where(age == years, jnp.float32(np.float32(0.7) ** years), stale)
    by_token = jnp.dot(
        jnp.concatenate([rows_of(adv[...], stale, dest_row, rank_row), gap[...]], axis=0),
        expand, precision=EXACT, preferred_element_type=jnp.float32,
    )
    pos = lax.rem(iota((seg, tokens), 1), seg)
    gap_row = jnp.sum(jnp.where(pos == iota((seg, tokens), 0), by_token[8:], 0.0), axis=0, keepdims=True)
    table[...] = lax.dot_general(
        rows_of(gap_row, *(by_token[i:i + 1] for i in range(4)), pos[0:1].astype(jnp.float32)),
        chosen_f32, (((1,), (1,)), ((), ())), precision=EXACT, preferred_element_type=jnp.float32,
    )


def unpack_hidden(packed, units, live_rows):
    tail, fold = fold_of(live_rows)
    short = units // fold
    pieces = tail * fold // 128
    wide = jnp.concatenate(
        [packed[units + j * short:units + (j + 1) * short].astype(jnp.float32) for j in range(pieces)], axis=1
    )
    folded = jnp.concatenate([wide[:, j * tail:(j + 1) * tail] for j in range(fold)], axis=0)
    return packed[:units], folded.astype(jnp.bfloat16)


def fetch(pieces, refs, held, sems, slots):
    copies = []
    quarters = sems.shape[1]
    live_rows, wide = held.shape[0] // len(slots), held.shape[1] // quarters
    for e in range(quarters):
        i = 0
        while i < len(slots):
            ref, at = pieces[slots[i], e]
            n = 1
            while ref and i + n < len(slots) and pieces[slots[i + n], e] == (ref, at + n):
                n += 1
            source = refs[ref].at[pl.ds(at * live_rows, n * live_rows)] if ref else refs[ref].at[at]
            target = held.at[pl.ds(i * live_rows, n * live_rows), pl.ds(e * wide, wide)]
            copies.append(pltpu.make_async_copy(source, target, sems.at[i, e]))
            copies[-1].start()
            i += n
    return copies


def shift_kernel(pieces, n_refs, slots, live_rows, weight, *rest):
    n = len(slots)
    hidden, refs, rest = rest[:n], rest[n:n + n_refs], rest[n + n_refs:]
    before, (sums, turned, held, rows_held, packed, sems, more_sems) = rest[:-7], rest[-7:]
    _, mp = my_place()
    quarters = sems.shape[1]
    units, width = weight.shape
    wide = width // quarters
    packed_copies, rows_copies = [], []
    for i in range(n):
        packed_copies.append(pltpu.make_async_copy(hidden[i], packed.at[i], more_sems.at[quarters + i]))
        packed_copies[i].start()
    for e in range(quarters):
        columns = pl.ds(pl.multiple_of((mp ^ e) * wide, 128), wide)
        rows_copies.append(
            pltpu.make_async_copy(weight.at[:, columns], rows_held.at[:, pl.ds(e * wide, wide)], more_sems.at[e])
        )
        rows_copies[e].start()
    copies = fetch(pieces, refs, held, sems, slots)
    for i in range(n):
        packed_copies[i].wait()
        head, tail = unpack_hidden(packed[i], units, live_rows)
        turned[:, i * live_rows:(i + 1) * live_rows] = jnp.concatenate([head, tail], axis=1)
    for e in range(quarters):
        rows_copies[e].wait()
    for copy in copies:
        copy.wait()
    product = lax.dot_general(
        rows_held[...], held[...], (((1,), (1,)), ((), ())), preferred_element_type=jnp.float32
    )
    line = jnp.sum(product * turned[...].astype(jnp.float32), axis=0, keepdims=True)
    total = before[0][...] if before else jnp.zeros(sums.shape, jnp.float32)
    row = iota(total.shape, 0)
    for i, k in enumerate(slots):
        total = jnp.where(row == k, line[:, i * live_rows:(i + 1) * live_rows], total)
    sums[...] = total


def by_slot(notes, which):
    slots = 2 * len(notes)
    out = jnp.zeros((slots, notes[0].shape[1]), jnp.float32)
    row = iota(out.shape, 0)
    for k in range(slots):
        at = slots + 8 * (k % 2) + which
        out = jnp.where(row == k, notes[k // 2][at:at + 1, :], out)
    return out


def swap_rows(values, m):
    row = iota(values.shape, 0)
    out = jnp.zeros_like(values)
    for k in range(values.shape[0]):
        out = jnp.where(row == k, values[k ^ m:(k ^ m) + 1, :], out)
    return out


def grad_kernel(pieces, n_refs, groups, slots_each, seglen, *rest):
    order = sum(groups, ())
    shards = len(order)
    hidden, rest = rest[:len(groups)], rest[len(groups):]
    refs, late_rows, rest = rest[:n_refs], rest[n_refs], rest[n_refs + 1:]
    notes, rest = rest[:shards // 2], rest[shards // 2:]
    ratio_out, grad_out, held, turned, scaled, result, sems, out_sems = rest
    dp, mp = my_place()
    quarters, wide = sems.shape[1], held.shape[1] // sems.shape[1]
    live_rows = notes[0].shape[1]
    copies = fetch(pieces, refs, held, sems, groups[0])
    scale = SCALE / math.sqrt(quarters * wide)
    at = 0
    for part in hidden:
        turned[:, at:at + part.shape[1]] = part[...]
        at += part.shape[1]

    total = notes[0][:shards]
    for i in range(1, len(notes)):
        total = total + swap_rows(notes[i][:shards], 2 * i)
    logit = by_slot(notes, GAP) + total * scale
    adv, dest = by_slot(notes, ADV), by_slot(notes, DEST)
    counts = jnp.zeros((shards, live_rows), jnp.float32)
    for shard in range(shards):
        here = dest == float(shard)
        tally = jnp.sum(jnp.sum(jnp.where(here, 1.0, 0.0), axis=1, keepdims=True), axis=0, keepdims=True)
        counts = jnp.where(here, tally, counts)
    ratio = jnp.exp(logit)
    squash = jnp.tanh((ratio - 1.0) / 0.2)
    clipped = 1.0 + 0.2 * squash
    slope = jnp.where(ratio * adv <= clipped * adv, 1.0, 1.0 - squash * squash)
    coef = -512.0 * by_slot(notes, STALE) * adv * ratio * slope / counts * scale

    eye = iota((live_rows, live_rows), 0) == iota((live_rows, live_rows), 1)
    columns = [jnp.sum(jnp.where(eye, coef[k:k + 1], 0.0), axis=1, keepdims=True) for k in order]

    def scale_rows(e):
        early = len(groups[0])
        for i in range(shards):
            source, at = (held, i) if i < early else (late_rows, i - early)
            part = source[at * live_rows:(at + 1) * live_rows, e * wide:(e + 1) * wide].astype(jnp.float32)
            scaled[e % 2, i * live_rows:(i + 1) * live_rows] = (columns[i] * part).astype(jnp.bfloat16)

    for copy in copies:
        copy.wait()
    writes = []
    scale_rows(0)
    for e in range(quarters):
        if e + 1 < quarters:
            scale_rows(e + 1)
        result[e] = jnp.dot(turned[...], scaled[e % 2], preferred_element_type=jnp.float32)
        write = pltpu.make_async_copy(
            result.at[e], grad_out.at[:, pl.ds(pl.multiple_of((mp ^ e) * wide, 128), wide)], out_sems.at[e]
        )
        write.start()
        writes.append(write)

    rank, pos = by_slot(notes, RANK), by_slot(notes, POS)
    spots = shards * slots_each
    spot = iota((spots, live_rows), 0).astype(jnp.float32)
    lane = iota((seglen, live_rows), 0).astype(jnp.float32)
    ratios = jnp.zeros((3 * seglen, spots), jnp.float32)
    for k in range(shards):
        to_me = dest[k:k + 1] == dp.astype(jnp.float32)
        target = ((dp ^ k) * slots_each).astype(jnp.float32) + rank[k:k + 1]
        left, spare = [], logit[k:k + 1]
        for _ in range(3):
            part = spare.astype(jnp.bfloat16).astype(jnp.float32)
            left.append(jnp.where(lane == pos[k:k + 1], part, 0.0))
            spare = spare - part
        ratios += lax.dot_general(
            jnp.concatenate(left, axis=0).astype(jnp.bfloat16),
            jnp.where((spot == target) & to_me, 1.0, 0.0).astype(jnp.bfloat16),
            (((1,), (1,)), ((), ())), preferred_element_type=jnp.float32,
        )
    ratio_out[...] = ratios[:seglen] + (ratios[seglen:2 * seglen] + ratios[2 * seglen:])
    for write in writes:
        write.wait()


MOVES = {
    "near": ("first", "dp", 2), "far": ("first", "dp", 6), "next": ("first", "dp", 4), "beside": ("both", "dp", 1),
    "x_n3": ("n3", "mp", 2), "y_n3": ("n3", "dp", 1), "xy_n3": ("y_n3", "mp", 2),
}
MOVES.update({f"h{k}": (f"pack{k}", "dp", k) for k in range(1, 8)})
HOLDS = {
    "beside": ((1, 0), (1, 2)), "n3": ((2, 0), (6, 0), (4, 0)), "y_n3": ((3, 0), (7, 0), (5, 0)),
    "x_n3": ((2, 2), (6, 2), (4, 2)), "xy_n3": ((3, 2), (7, 2), (5, 2)),
}
MOVES.update({"c_" + name: (name, "mp", 1) for name in HOLDS})
PLAN = (
    ("far", "next", "near", "beside", "rest", "h1",),
    ("x_n3", "y_n3", "h4", "h6", "c_beside", "c_n3",),
    ("xy_n3", "h7", "h5", "h3", "h2", "c_x_n3", "c_y_n3", "early",),
    ("c_xy_n3",),
)
BESIDES = {"h3": ("c_y_n3",), "early": ("h7",), "c_xy_n3": ("early",)}
FREE = ()
EARLY = (0, 1, 2, 6, 4, )
LATE = (3, 7, 5, )


def cube_body(hidden_act, readout, log_gap, advantage, version, lengths, routes, weight):
    shards, quarters = lax.axis_size("dp"), lax.axis_size("mp")
    respond, seglen = log_gap.shape
    live_rows = 7 * respond * seglen // 8
    width = readout.shape[1]
    wide = width // quarters
    units = weight.shape[0]
    rows = packed_rows(units, live_rows)
    slots_each = 2 * respond // shards
    bf16, f32 = jnp.bfloat16, jnp.float32
    def room(mib):
        return pltpu.CompilerParams(vmem_limit_bytes=mib * 1024 * 1024)

    def cost(flops, moved):
        return pl.CostEstimate(flops=int(flops), bytes_accessed=int(moved), transcendentals=0)

    def over_dp(x, m):
        return lax.ppermute(x, "dp", [(s, s ^ m) for s in range(shards)])

    def over_mp(x, m):
        return lax.ppermute(x, "mp", [(s, s ^ m) for s in range(quarters)])

    def over_both(x, m, h):
        pairs = [(s * quarters + t, (s ^ m) * quarters + (t ^ h)) for s in range(shards) for t in range(quarters)]
        return lax.ppermute(x, ("dp", "mp"), pairs)

    got = {}

    def after(x, names):
        names = [name for name in names if name in got]
        return lax.optimization_barrier((x, *(got[name] for name in names)))[0] if names else x

    got["first"], got["both"] = pl.pallas_call(
        functools.partial(pack_first, live_rows, seglen),
        out_shape=(jax.ShapeDtypeStruct((live_rows, wide), bf16), jax.ShapeDtypeStruct((2 * live_rows, wide), bf16)),
        in_specs=[VMEM, ANY],
        out_specs=(VMEM, VMEM),
        scratch_shapes=[pltpu.VMEM((2, respond * seglen, wide), bf16), pltpu.SemaphoreType.DMA((2,))],
        compiler_params=room(12),
        name="pack_first",
    )(lengths, readout)

    def rest(gates):
        table, own, *hidden = pl.pallas_call(
            functools.partial(pack_rest, live_rows, seglen),
            out_shape=(
                jax.ShapeDtypeStruct((8, live_rows), f32),
                jax.ShapeDtypeStruct((quarters, live_rows, wide), bf16),
            ) + (jax.ShapeDtypeStruct((rows, 128), bf16),) * shards,
            in_specs=[VMEM] * 7,
            out_specs=(VMEM,) * (shards + 2),
            scratch_shapes=[pltpu.VMEM((shards * rows, 128), bf16)],
            compiler_params=room(20),
            cost_estimate=cost(2e9, 8e6),
            name="pack_rest",
        )(after(lengths, gates), routes.reshape(1, respond), log_gap.T, advantage.reshape(1, respond),
          version.reshape(1, respond), readout, hidden_act)
        got.update({"table": table, "own": own, "h0": hidden[0], "rest": table})
        got.update({f"pack{k}": hidden[k] for k in range(1, shards)})

    def used(slots):
        names, places = ["own"], {(0, e): (0, e) for e in range(quarters)}
        for name, blocks in HOLDS.items():
            for core in (0, 1):
                if any(k in slots for k, _ in blocks):
                    for block, (k, e) in enumerate(blocks):
                        places[k, e ^ core] = (len(names), block)
                    names.append("c_" + name if core else name)
        return [got[name] for name in names], places

    groups = (EARLY, LATE)
    turned, late_rows = [], []

    def shift_sums(slots, *before, gates=(), keep=False):
        refs, places = used(slots)
        refs[0] = after(refs[0], gates)
        rows_shape = (len(slots) * live_rows, width)
        sums, part, *kept = pl.pallas_call(
            functools.partial(shift_kernel, places, len(refs), slots, live_rows),
            out_shape=(
                jax.ShapeDtypeStruct((shards, live_rows), f32),
                jax.ShapeDtypeStruct((units, len(slots) * live_rows), bf16),
            ) + (jax.ShapeDtypeStruct(rows_shape, bf16),) * keep,
            in_specs=[ANY] * (1 + len(slots) + len(refs)) + [VMEM] * len(before),
            out_specs=(VMEM,) * (2 + keep),
            scratch_shapes=[pltpu.VMEM(rows_shape, bf16)] * (not keep) + [
                pltpu.VMEM((units, width), bf16),
                pltpu.VMEM((len(slots), rows, 128), bf16),
                pltpu.SemaphoreType.DMA((len(slots), quarters)),
                pltpu.SemaphoreType.DMA((quarters + len(slots),)),
            ],
            compiler_params=room(20),
            cost_estimate=cost(2 * units * len(slots) * live_rows * width, 2 * len(slots) * live_rows * width),
            name="shift_sums",
        )(weight, *(got[f"h{k}"] for k in slots), *refs, *before)
        turned.append(part)
        late_rows.extend(kept)
        return sums

    gates = ()
    for steps in PLAN:
        moved = []
        for step in steps:
            if step == "rest":
                rest(gates)
                moved.append(step)
            elif step == "early":
                got[step] = shift_sums(EARLY, gates=BESIDES.get(step, ()))
            else:
                source, axis, m = MOVES[step]
                if source == "n3" and source not in got:
                    got[source] = jnp.concatenate([got["near"], got["far"], got["next"]], axis=0)
                core = [name for name in moved if name[:2] == "c_" and step[:2] == "c_"]
                got[step] = (over_dp if axis == "dp" else over_mp)(
                    after(got[source], (*gates, *core, *BESIDES.get(step, ()))), m
                )
                if step not in FREE:
                    moved.append(step)
        gates = tuple(moved)
    sums = shift_sums(LATE, got["early"], keep=True)

    sums = sums + over_mp(sums, 1)
    table = got["table"]
    beside = over_dp(jnp.concatenate([sums, table], axis=0), 1)
    across = beside[:shards] + over_both(sums, 1, 2)
    sums = sums + over_mp(sums, 2)
    note = jnp.concatenate(
        [sums + jnp.concatenate([across[k ^ 1:(k ^ 1) + 1] for k in range(shards)], axis=0), table, beside[shards:]], axis=0
    )
    notes = [note] + [over_dp(note, m) for m in (2, 4, 6)]

    refs, places = used(EARLY)
    log_ratio, weight_grad = pl.pallas_call(
        functools.partial(grad_kernel, places, len(refs), groups, slots_each, seglen),
        out_shape=(
            jax.ShapeDtypeStruct((seglen, shards * slots_each), f32),
            jax.ShapeDtypeStruct((units, width), f32),
        ),
        in_specs=[VMEM] * len(groups) + [ANY] * len(refs) + [VMEM] * (1 + len(notes)),
        out_specs=(VMEM, ANY),
        scratch_shapes=[
            pltpu.VMEM((len(EARLY) * live_rows, width), bf16),
            pltpu.VMEM((units, shards * live_rows), bf16),
            pltpu.VMEM((2, shards * live_rows, wide), bf16),
            pltpu.VMEM((quarters, units, wide), f32),
            pltpu.SemaphoreType.DMA((len(EARLY), quarters)),
            pltpu.SemaphoreType.DMA((quarters,)),
        ],
        compiler_params=room(52),
        cost_estimate=cost(2 * units * shards * live_rows * width, 2 * shards * live_rows * width + 4 * units * width),
        name="weight_grad",
    )(*turned, *refs, *late_rows, *notes)
    return (log_ratio.T, weight_grad)


def general_body(hidden_act, readout, log_gap, advantage, version, lengths, routes, weight):
    shards = lax.axis_size("dp")
    respond, seglen = log_gap.shape
    tokens = respond * seglen
    live_rows = 7 * tokens // 8
    width = readout.shape[1]
    units = weight.shape[0]
    slots = 2 * respond // shards
    scale = SCALE / math.sqrt(width)
    f32 = jnp.float32
    dest = routes[:, 0]
    onehot = (dest[:, None] == jnp.arange(shards, dtype=jnp.int32)[None, :]).astype(jnp.int32)
    rank = jnp.sum((jnp.cumsum(onehot, axis=0) - onehot) * onehot, axis=1)
    lens = lengths[0]
    live = (jnp.arange(seglen, dtype=jnp.int32)[None, :] < lens[:, None]).reshape(-1)
    order = jnp.cumsum(live.astype(jnp.int32)) - 1
    select = live[None, :] & (order[None, :] == jnp.arange(live_rows, dtype=jnp.int32)[:, None])
    hidden = jnp.dot(select.astype(jnp.bfloat16), hidden_act)
    hidden = lax.all_to_all(
        hidden.reshape(live_rows, shards, units).swapaxes(0, 1), "dp", split_axis=0, concat_axis=0
    )
    read = lax.all_gather(jnp.dot(select.astype(jnp.bfloat16), readout), "dp", axis=0)

    def one_sum(k, sums):
        product = lax.dot_general(read[k], weight, (((1,), (1,)), ((), ())), preferred_element_type=f32)
        return sums.at[k].set(jnp.sum(product * hidden[k].astype(f32), axis=1))

    sums = lax.fori_loop(0, shards, one_sum, jnp.zeros((shards, live_rows), f32))
    sums = lax.psum(lax.psum_scatter(sums, "dp", scatter_dimension=0, tiled=True)[0], "mp")
    shift = jnp.dot(sums[None, :], select.astype(f32), precision=EXACT).reshape(respond, seglen) * scale
    logit = log_gap + shift
    live = live.reshape(respond, seglen)
    onehot_float = onehot.astype(f32)
    shard_count = lax.psum(jnp.sum(onehot_float * lens.astype(f32)[:, None], axis=0), "dp")
    count_each = jnp.sum(onehot_float * shard_count[None, :], axis=1)
    stale = jnp.power(jnp.float32(0.7), (NVER - 1 - version).astype(f32))
    send = jnp.arange(shards * slots, dtype=jnp.int32)[:, None] == (dest * slots + rank)[None, :]
    log_ratio = lax.all_to_all(
        jnp.dot(send.astype(f32), jnp.where(live, logit, 0.0), precision=EXACT),
        "dp", split_axis=0, concat_axis=0, tiled=True,
    )
    ratio = jnp.exp(logit)
    squash = jnp.tanh((ratio - 1.0) / 0.2)
    clipped = 1.0 + 0.2 * squash
    adv = advantage[:, None]
    slope = jnp.where(ratio * adv <= clipped * adv, 1.0, 1.0 - squash * squash)
    coef = jnp.where(live, -512.0 * stale[:, None] * adv * ratio * slope / count_each[:, None], 0.0)
    coef = jnp.dot(select.astype(f32), coef.reshape(-1, 1), precision=EXACT)[:, 0]
    coefs = lax.all_gather(coef, "dp", axis=0)

    def one_term(k, grad):
        out_grad = (coefs[k][:, None] * scale * read[k].astype(f32)).astype(jnp.bfloat16)
        return grad + lax.dot_general(
            hidden[k], out_grad, (((0,), (0,)), ((), ())), preferred_element_type=f32
        )

    return (log_ratio, lax.fori_loop(0, shards, one_term, jnp.zeros((units, width), f32)))


def body(*args):
    if lax.axis_size("dp") == 8 and lax.axis_size("mp") == 4:
        return cube_body(*args)
    return general_body(*args)


def solution(mesh):
    placed = (
        P("dp", "mp"),
        P("dp", None),
        P("dp", None),
        P("dp"),
        P("dp"),
        P("dp", None),
        P("dp", None),
        P(("mp", "dp"), None),
    )
    return jax.shard_map(
        body,
        mesh=mesh,
        in_specs=placed,
        out_specs=(P("dp", None), P(("mp", "dp"), None)),
        check_vma=False,
    )
```

```python
import functools
import math

import jax
import jax.numpy as jnp
import numpy as np
from jax import lax
from jax.experimental import pallas as pl
from jax.experimental.pallas import tpu as pltpu
from jax.sharding import PartitionSpec as P

NVER = 4
SCALE = 0.15
EXACT = lax.Precision.HIGHEST
VMEM = pl.BlockSpec(memory_space=pltpu.VMEM)
SMEM = pl.BlockSpec(memory_space=pltpu.SMEM)
ANY = pl.BlockSpec(memory_space=pl.ANY)
GAP, ADV, STALE, DEST, RANK, POS = range(6)


def iota(shape, axis):
    return lax.broadcasted_iota(jnp.int32, shape, axis)


def rows_of(*rows):
    n = rows[0].shape[1]
    row = iota((8, n), 0)
    table = jnp.zeros((8, n), jnp.float32)
    for i, values in enumerate(rows):
        table = jnp.where(row == i, values, table)
    return table


def my_place():
    return lax.axis_index("dp"), lax.axis_index("mp")


def live_tokens(live_rows, seglen, lens):
    respond = lens.shape[1]
    tokens = respond * seglen
    expand = (iota((respond, tokens), 0) == lax.div(iota((respond, tokens), 1), seglen)).astype(jnp.bfloat16)
    lens_wide = jnp.broadcast_to(lens.astype(jnp.float32), (16, respond)).astype(jnp.bfloat16)
    by_token = jnp.dot(lens_wide, expand, preferred_element_type=jnp.float32)
    live = lax.rem(iota((16, tokens), 1), seglen).astype(jnp.float32) < by_token
    before = (iota((tokens, tokens), 0) < iota((tokens, tokens), 1)).astype(jnp.bfloat16)
    order = jnp.dot(live.astype(jnp.float32).astype(jnp.bfloat16), before, preferred_element_type=jnp.float32)
    place = jnp.where(live, order, -1.0)[0:1, :]
    return place == iota((live_rows, tokens), 0).astype(jnp.float32)


def pack_first(live_rows, seglen, lens, read, first, both, held, sems):
    _, mp = my_place()
    wide = held.shape[2]
    copies = []
    for i, e in enumerate((0, 2)):
        columns = pl.ds(pl.multiple_of((mp ^ e) * wide, 128), wide)
        copies.append(pltpu.make_async_copy(read.at[:, columns], held.at[i], sems.at[i]))
        copies[-1].start()
    select = live_tokens(live_rows, seglen, lens[...]).astype(jnp.float32).astype(jnp.bfloat16)
    for i in range(2):
        copies[i].wait()
        part = jnp.dot(select, held[i], preferred_element_type=jnp.float32).astype(jnp.bfloat16)
        both[i * live_rows:(i + 1) * live_rows] = part
        if i == 0:
            first[...] = part


def packed_rows(units, live_rows):
    return units * live_rows // 128


def fold_of(live_rows):
    tail = live_rows - 128
    return tail, 128 // math.gcd(tail, 128)


def pack_rest(live_rows, seglen, lens, routes, gap, adv, version, read, hidden, *rest):
    table, own, outs, held = rest[0], rest[1], rest[2:-1], rest[-1]
    dp, mp = my_place()
    seg, respond = gap.shape
    tokens = respond * seg
    chosen = live_tokens(live_rows, seglen, lens[...])
    chosen_f32 = chosen.astype(jnp.float32)
    select = chosen_f32.astype(jnp.bfloat16)
    units = hidden.shape[1] // len(outs)
    tail, fold = fold_of(live_rows)
    short = units // fold
    pieces = tail * fold // 128
    rows = packed_rows(units, live_rows)
    for block in range(0, len(outs), 2):
        turned = lax.dot_general(
            hidden[:, block * units:(block + 2) * units], select, (((0,), (1,)), ((), ())),
            preferred_element_type=jnp.float32,
        )
        for i in range(2):
            part = turned[i * units:(i + 1) * units]
            at = (block + i) * rows
            held[at:at + units] = part[:, :128].astype(jnp.bfloat16)
            wide = jnp.concatenate([part[j * short:(j + 1) * short, 128:] for j in range(fold)], axis=1)
            for j in range(pieces):
                start = at + units + j * short
                held[start:start + short] = wide[:, j * 128:(j + 1) * 128].astype(jnp.bfloat16)
    for k, out in enumerate(outs):
        out[...] = held[pl.ds(pl.multiple_of((dp ^ k) * rows, 16), rows)]

    wide = read.shape[1] // own.shape[0]
    for quarter in range(own.shape[0]):
        own[mp ^ quarter] = jnp.dot(
            select, read[:, quarter * wide:(quarter + 1) * wide], preferred_element_type=jnp.float32
        ).astype(jnp.bfloat16)

    expand = (iota((respond, tokens), 0) == lax.div(iota((respond, tokens), 1), seg)).astype(jnp.float32)
    eye = iota((respond, respond), 0) == iota((respond, respond), 1)
    dest_row = routes[...].astype(jnp.float32)
    dest_col = jnp.sum(jnp.where(eye, dest_row, 0.0), axis=1, keepdims=True)
    earlier = (dest_col == dest_row) & (iota((respond, respond), 0) < iota((respond, respond), 1))
    rank_row = jnp.sum(jnp.where(earlier, 1.0, 0.0), axis=0, keepdims=True)
    age = NVER - 1 - version[...]
    stale = jnp.ones(age.shape, jnp.float32)
    for years in range(1, NVER):
        stale = jnp.where(age == years, jnp.float32(np.float32(0.7) ** years), stale)
    by_token = jnp.dot(
        jnp.concatenate([rows_of(adv[...], stale, dest_row, rank_row), gap[...]], axis=0),
        expand, precision=EXACT, preferred_element_type=jnp.float32,
    )
    pos = lax.rem(iota((seg, tokens), 1), seg)
    gap_row = jnp.sum(jnp.where(pos == iota((seg, tokens), 0), by_token[8:], 0.0), axis=0, keepdims=True)
    table[...] = lax.dot_general(
        rows_of(gap_row, *(by_token[i:i + 1] for i in range(4)), pos[0:1].astype(jnp.float32)),
        chosen_f32, (((1,), (1,)), ((), ())), precision=EXACT, preferred_element_type=jnp.float32,
    )


def unpack_hidden(packed, units, live_rows):
    tail, fold = fold_of(live_rows)
    short = units // fold
    pieces = tail * fold // 128
    wide = jnp.concatenate(
        [packed[units + j * short:units + (j + 1) * short].astype(jnp.float32) for j in range(pieces)], axis=1
    )
    folded = jnp.concatenate([wide[:, j * tail:(j + 1) * tail] for j in range(fold)], axis=0)
    return packed[:units], folded.astype(jnp.bfloat16)


def fetch(pieces, refs, held, sems, slots):
    copies = []
    quarters = sems.shape[1]
    live_rows, wide = held.shape[0] // len(slots), held.shape[1] // quarters
    for e in range(quarters):
        i = 0
        while i < len(slots):
            ref, at = pieces[slots[i], e]
            n = 1
            while ref and i + n < len(slots) and pieces[slots[i + n], e] == (ref, at + n):
                n += 1
            source = refs[ref].at[pl.ds(at * live_rows, n * live_rows)] if ref else refs[ref].at[at]
            target = held.at[pl.ds(i * live_rows, n * live_rows), pl.ds(e * wide, wide)]
            copies.append(pltpu.make_async_copy(source, target, sems.at[i, e]))
            copies[-1].start()
            i += n
    return copies


def shift_kernel(pieces, n_refs, slots, live_rows, weight, *rest):
    n = len(slots)
    hidden, refs, rest = rest[:n], rest[n:n + n_refs], rest[n + n_refs:]
    before, (sums, turned, held, rows_held, packed, sems, more_sems) = rest[:-7], rest[-7:]
    _, mp = my_place()
    quarters = sems.shape[1]
    units, width = weight.shape
    wide = width // quarters
    copies = fetch(pieces, refs, held, sems, slots)
    packed_copies, rows_copies = [], []
    for i in range(n):
        packed_copies.append(pltpu.make_async_copy(hidden[i], packed.at[i], more_sems.at[quarters + i]))
        packed_copies[i].start()
    for e in range(quarters):
        columns = pl.ds(pl.multiple_of((mp ^ e) * wide, 128), wide)
        rows_copies.append(
            pltpu.make_async_copy(weight.at[:, columns], rows_held.at[:, pl.ds(e * wide, wide)], more_sems.at[e])
        )
        rows_copies[e].start()
    for i in range(n):
        packed_copies[i].wait()
        head, tail = unpack_hidden(packed[i], units, live_rows)
        turned[:, i * live_rows:(i + 1) * live_rows] = jnp.concatenate([head, tail], axis=1)
    for e in range(quarters):
        rows_copies[e].wait()
    for copy in copies:
        copy.wait()
    product = lax.dot_general(
        rows_held[...], held[...], (((1,), (1,)), ((), ())), preferred_element_type=jnp.float32
    )
    line = jnp.sum(product * turned[...].astype(jnp.float32), axis=0, keepdims=True)
    total = before[0][...] if before else jnp.zeros(sums.shape, jnp.float32)
    row = iota(total.shape, 0)
    for i, k in enumerate(slots):
        total = jnp.where(row == k, line[:, i * live_rows:(i + 1) * live_rows], total)
    sums[...] = total


def by_slot(notes, which):
    slots = 2 * len(notes)
    out = jnp.zeros((slots, notes[0].shape[1]), jnp.float32)
    row = iota(out.shape, 0)
    for k in range(slots):
        at = slots + 8 * (k % 2) + which
        out = jnp.where(row == k, notes[k // 2][at:at + 1, :], out)
    return out


def swap_rows(values, m):
    row = iota(values.shape, 0)
    out = jnp.zeros_like(values)
    for k in range(values.shape[0]):
        out = jnp.where(row == k, values[k ^ m:(k ^ m) + 1, :], out)
    return out


def grad_kernel(pieces, n_refs, groups, slots_each, seglen, *rest):
    order = sum(groups, ())
    shards = len(order)
    hidden, rest = rest[:len(groups)], rest[len(groups):]
    refs, late_rows, rest = rest[:n_refs], rest[n_refs], rest[n_refs + 1:]
    notes, rest = rest[:shards // 2], rest[shards // 2:]
    ratio_out, grad_out, held, turned, scaled, result, sems, out_sems = rest
    dp, mp = my_place()
    quarters, wide = sems.shape[1], held.shape[1] // sems.shape[1]
    live_rows = notes[0].shape[1]
    copies = fetch(pieces, refs, held, sems, groups[0])
    scale = SCALE / math.sqrt(quarters * wide)
    at = 0
    for part in hidden:
        turned[:, at:at + part.shape[1]] = part[...]
        at += part.shape[1]

    total = notes[0][:shards]
    for i in range(1, len(notes)):
        total = total + swap_rows(notes[i][:shards], 2 * i)
    logit = by_slot(notes, GAP) + total * scale
    adv, dest = by_slot(notes, ADV), by_slot(notes, DEST)
    counts = jnp.zeros((shards, live_rows), jnp.float32)
    for shard in range(shards):
        here = dest == float(shard)
        tally = jnp.sum(jnp.sum(jnp.where(here, 1.0, 0.0), axis=1, keepdims=True), axis=0, keepdims=True)
        counts = jnp.where(here, tally, counts)
    ratio = jnp.exp(logit)
    squash = jnp.tanh((ratio - 1.0) / 0.2)
    clipped = 1.0 + 0.2 * squash
    slope = jnp.where(ratio * adv <= clipped * adv, 1.0, 1.0 - squash * squash)
    coef = -512.0 * by_slot(notes, STALE) * adv * ratio * slope / counts * scale

    eye = iota((live_rows, live_rows), 0) == iota((live_rows, live_rows), 1)
    columns = [jnp.sum(jnp.where(eye, coef[k:k + 1], 0.0), axis=1, keepdims=True) for k in order]

    def scale_rows(e):
        early = len(groups[0])
        for i in range(shards):
            source, at = (held, i) if i < early else (late_rows, i - early)
            part = source[at * live_rows:(at + 1) * live_rows, e * wide:(e + 1) * wide].astype(jnp.float32)
            scaled[e % 2, i * live_rows:(i + 1) * live_rows] = (columns[i] * part).astype(jnp.bfloat16)

    for copy in copies:
        copy.wait()
    writes = []
    scale_rows(0)
    for e in range(quarters):
        if e + 1 < quarters:
            scale_rows(e + 1)
        result[e] = jnp.dot(turned[...], scaled[e % 2], preferred_element_type=jnp.float32)
        write = pltpu.make_async_copy(
            result.at[e], grad_out.at[:, pl.ds(pl.multiple_of((mp ^ e) * wide, 128), wide)], out_sems.at[e]
        )
        write.start()
        writes.append(write)

    rank, pos = by_slot(notes, RANK), by_slot(notes, POS)
    spots = shards * slots_each
    spot = iota((spots, live_rows), 0).astype(jnp.float32)
    lane = iota((seglen, live_rows), 0).astype(jnp.float32)
    ratios = jnp.zeros((3 * seglen, spots), jnp.float32)
    for k in range(shards):
        to_me = dest[k:k + 1] == dp.astype(jnp.float32)
        target = ((dp ^ k) * slots_each).astype(jnp.float32) + rank[k:k + 1]
        left, spare = [], logit[k:k + 1]
        for _ in range(3):
            part = spare.astype(jnp.bfloat16).astype(jnp.float32)
            left.append(jnp.where(lane == pos[k:k + 1], part, 0.0))
            spare = spare - part
        ratios += lax.dot_general(
            jnp.concatenate(left, axis=0).astype(jnp.bfloat16),
            jnp.where((spot == target) & to_me, 1.0, 0.0).astype(jnp.bfloat16),
            (((1,), (1,)), ((), ())), preferred_element_type=jnp.float32,
        )
    ratio_out[...] = ratios[:seglen] + (ratios[seglen:2 * seglen] + ratios[2 * seglen:])
    for write in writes:
        write.wait()


MOVES = {
    "near": ("first", "dp", 2), "far": ("first", "dp", 6), "next": ("first", "dp", 4), "beside": ("both", "dp", 1),
    "x_n3": ("n3", "mp", 2), "y_n3": ("n3", "dp", 1), "xy_n3": ("y_n3", "mp", 2),
}
MOVES.update({f"h{k}": (f"pack{k}", "dp", k) for k in range(1, 8)})
HOLDS = {
    "beside": ((1, 0), (1, 2)), "n3": ((2, 0), (6, 0), (4, 0)), "y_n3": ((3, 0), (7, 0), (5, 0)),
    "x_n3": ((2, 2), (6, 2), (4, 2)), "xy_n3": ((3, 2), (7, 2), (5, 2)),
}
MOVES.update({"c_" + name: (name, "mp", 1) for name in HOLDS})
PLAN = (
    ("far", "next", "near", "beside", "rest", "h1",),
    ("x_n3", "y_n3", "h4", "h6", "c_beside", "c_n3",),
    ("xy_n3", "h7", "h5", "h3", "h2", "c_x_n3", "c_y_n3", "early",),
    ("c_xy_n3",),
)
BESIDES = {"h3": ("c_y_n3",), "early": ("h7",), "c_xy_n3": ("early",)}
FREE = ()
EARLY = (0, 1, 2, 6, 4, )
LATE = (3, 7, 5, )


def cube_body(hidden_act, readout, log_gap, advantage, version, lengths, routes, weight):
    shards, quarters = lax.axis_size("dp"), lax.axis_size("mp")
    respond, seglen = log_gap.shape
    live_rows = 7 * respond * seglen // 8
    width = readout.shape[1]
    wide = width // quarters
    units = weight.shape[0]
    rows = packed_rows(units, live_rows)
    slots_each = 2 * respond // shards
    bf16, f32 = jnp.bfloat16, jnp.float32
    def room(mib):
        return pltpu.CompilerParams(vmem_limit_bytes=mib * 1024 * 1024)

    def cost(flops, moved):
        return pl.CostEstimate(flops=int(flops), bytes_accessed=int(moved), transcendentals=0)

    def over_dp(x, m):
        return lax.ppermute(x, "dp", [(s, s ^ m) for s in range(shards)])

    def over_mp(x, m):
        return lax.ppermute(x, "mp", [(s, s ^ m) for s in range(quarters)])

    def over_both(x, m, h):
        pairs = [(s * quarters + t, (s ^ m) * quarters + (t ^ h)) for s in range(shards) for t in range(quarters)]
        return lax.ppermute(x, ("dp", "mp"), pairs)

    got = {}

    def after(x, names):
        names = [name for name in names if name in got]
        return lax.optimization_barrier((x, *(got[name] for name in names)))[0] if names else x

    got["first"], got["both"] = pl.pallas_call(
        functools.partial(pack_first, live_rows, seglen),
        out_shape=(jax.ShapeDtypeStruct((live_rows, wide), bf16), jax.ShapeDtypeStruct((2 * live_rows, wide), bf16)),
        in_specs=[VMEM, ANY],
        out_specs=(VMEM, VMEM),
        scratch_shapes=[pltpu.VMEM((2, respond * seglen, wide), bf16), pltpu.SemaphoreType.DMA((2,))],
        compiler_params=room(12),
        name="pack_first",
    )(lengths, readout)

    def rest(gates):
        table, own, *hidden = pl.pallas_call(
            functools.partial(pack_rest, live_rows, seglen),
            out_shape=(
                jax.ShapeDtypeStruct((8, live_rows), f32),
                jax.ShapeDtypeStruct((quarters, live_rows, wide), bf16),
            ) + (jax.ShapeDtypeStruct((rows, 128), bf16),) * shards,
            in_specs=[VMEM] * 7,
            out_specs=(VMEM,) * (shards + 2),
            scratch_shapes=[pltpu.VMEM((shards * rows, 128), bf16)],
            compiler_params=room(20),
            cost_estimate=cost(2e9, 8e6),
            name="pack_rest",
        )(after(lengths, gates), routes.reshape(1, respond), log_gap.T, advantage.reshape(1, respond),
          version.reshape(1, respond), readout, hidden_act)
        got.update({"table": table, "own": own, "h0": hidden[0], "rest": table})
        got.update({f"pack{k}": hidden[k] for k in range(1, shards)})

    def used(slots):
        names, places = ["own"], {(0, e): (0, e) for e in range(quarters)}
        for name, blocks in HOLDS.items():
            for core in (0, 1):
                if any(k in slots for k, _ in blocks):
                    for block, (k, e) in enumerate(blocks):
                        places[k, e ^ core] = (len(names), block)
                    names.append("c_" + name if core else name)
        return [got[name] for name in names], places

    groups = (EARLY, LATE)
    turned, late_rows = [], []

    def shift_sums(slots, *before, gates=(), keep=False):
        refs, places = used(slots)
        refs[0] = after(refs[0], gates)
        rows_shape = (len(slots) * live_rows, width)
        sums, part, *kept = pl.pallas_call(
            functools.partial(shift_kernel, places, len(refs), slots, live_rows),
            out_shape=(
                jax.ShapeDtypeStruct((shards, live_rows), f32),
                jax.ShapeDtypeStruct((units, len(slots) * live_rows), bf16),
            ) + (jax.ShapeDtypeStruct(rows_shape, bf16),) * keep,
            in_specs=[ANY] * (1 + len(slots) + len(refs)) + [VMEM] * len(before),
            out_specs=(VMEM,) * (2 + keep),
            scratch_shapes=[pltpu.VMEM(rows_shape, bf16)] * (not keep) + [
                pltpu.VMEM((units, width), bf16),
                pltpu.VMEM((len(slots), rows, 128), bf16),
                pltpu.SemaphoreType.DMA((len(slots), quarters)),
                pltpu.SemaphoreType.DMA((quarters + len(slots),)),
            ],
            compiler_params=room(20),
            cost_estimate=cost(2 * units * len(slots) * live_rows * width, 2 * len(slots) * live_rows * width),
            name="shift_sums",
        )(weight, *(got[f"h{k}"] for k in slots), *refs, *before)
        turned.append(part)
        late_rows.extend(kept)
        return sums

    gates = ()
    for steps in PLAN:
        moved = []
        for step in steps:
            if step == "rest":
                rest(gates)
                moved.append(step)
            elif step == "early":
                got[step] = shift_sums(EARLY, gates=BESIDES.get(step, ()))
            else:
                source, axis, m = MOVES[step]
                if source == "n3" and source not in got:
                    got[source] = jnp.concatenate([got["near"], got["far"], got["next"]], axis=0)
                core = [name for name in moved if name[:2] == "c_" and step[:2] == "c_"]
                got[step] = (over_dp if axis == "dp" else over_mp)(
                    after(got[source], (*gates, *core, *BESIDES.get(step, ()))), m
                )
                if step not in FREE:
                    moved.append(step)
        gates = tuple(moved)
    sums = shift_sums(LATE, got["early"], keep=True)

    sums = sums + over_mp(sums, 1)
    table = got["table"]
    beside = over_dp(jnp.concatenate([sums, table], axis=0), 1)
    across = beside[:shards] + over_both(sums, 1, 2)
    sums = sums + over_mp(sums, 2)
    note = jnp.concatenate(
        [sums + jnp.concatenate([across[k ^ 1:(k ^ 1) + 1] for k in range(shards)], axis=0), table, beside[shards:]], axis=0
    )
    notes = [note] + [over_dp(note, m) for m in (2, 4, 6)]

    refs, places = used(EARLY)
    log_ratio, weight_grad = pl.pallas_call(
        functools.partial(grad_kernel, places, len(refs), groups, slots_each, seglen),
        out_shape=(
            jax.ShapeDtypeStruct((seglen, shards * slots_each), f32),
            jax.ShapeDtypeStruct((units, width), f32),
        ),
        in_specs=[VMEM] * len(groups) + [ANY] * len(refs) + [VMEM] * (1 + len(notes)),
        out_specs=(VMEM, ANY),
        scratch_shapes=[
            pltpu.VMEM((len(EARLY) * live_rows, width), bf16),
            pltpu.VMEM((units, shards * live_rows), bf16),
            pltpu.VMEM((2, shards * live_rows, wide), bf16),
            pltpu.VMEM((quarters, units, wide), f32),
            pltpu.SemaphoreType.DMA((len(EARLY), quarters)),
            pltpu.SemaphoreType.DMA((quarters,)),
        ],
        compiler_params=room(52),
        cost_estimate=cost(2 * units * shards * live_rows * width, 2 * shards * live_rows * width + 4 * units * width),
        name="weight_grad",
    )(*turned, *refs, *late_rows, *notes)
    return (log_ratio.T, weight_grad)


def general_body(hidden_act, readout, log_gap, advantage, version, lengths, routes, weight):
    shards = lax.axis_size("dp")
    respond, seglen = log_gap.shape
    tokens = respond * seglen
    live_rows = 7 * tokens // 8
    width = readout.shape[1]
    units = weight.shape[0]
    slots = 2 * respond // shards
    scale = SCALE / math.sqrt(width)
    f32 = jnp.float32
    dest = routes[:, 0]
    onehot = (dest[:, None] == jnp.arange(shards, dtype=jnp.int32)[None, :]).astype(jnp.int32)
    rank = jnp.sum((jnp.cumsum(onehot, axis=0) - onehot) * onehot, axis=1)
    lens = lengths[0]
    live = (jnp.arange(seglen, dtype=jnp.int32)[None, :] < lens[:, None]).reshape(-1)
    order = jnp.cumsum(live.astype(jnp.int32)) - 1
    select = live[None, :] & (order[None, :] == jnp.arange(live_rows, dtype=jnp.int32)[:, None])
    hidden = jnp.dot(select.astype(jnp.bfloat16), hidden_act)
    hidden = lax.all_to_all(
        hidden.reshape(live_rows, shards, units).swapaxes(0, 1), "dp", split_axis=0, concat_axis=0
    )
    read = lax.all_gather(jnp.dot(select.astype(jnp.bfloat16), readout), "dp", axis=0)

    def one_sum(k, sums):
        product = lax.dot_general(read[k], weight, (((1,), (1,)), ((), ())), preferred_element_type=f32)
        return sums.at[k].set(jnp.sum(product * hidden[k].astype(f32), axis=1))

    sums = lax.fori_loop(0, shards, one_sum, jnp.zeros((shards, live_rows), f32))
    sums = lax.psum(lax.psum_scatter(sums, "dp", scatter_dimension=0, tiled=True)[0], "mp")
    shift = jnp.dot(sums[None, :], select.astype(f32), precision=EXACT).reshape(respond, seglen) * scale
    logit = log_gap + shift
    live = live.reshape(respond, seglen)
    onehot_float = onehot.astype(f32)
    shard_count = lax.psum(jnp.sum(onehot_float * lens.astype(f32)[:, None], axis=0), "dp")
    count_each = jnp.sum(onehot_float * shard_count[None, :], axis=1)
    stale = jnp.power(jnp.float32(0.7), (NVER - 1 - version).astype(f32))
    send = jnp.arange(shards * slots, dtype=jnp.int32)[:, None] == (dest * slots + rank)[None, :]
    log_ratio = lax.all_to_all(
        jnp.dot(send.astype(f32), jnp.where(live, logit, 0.0), precision=EXACT),
        "dp", split_axis=0, concat_axis=0, tiled=True,
    )
    ratio = jnp.exp(logit)
    squash = jnp.tanh((ratio - 1.0) / 0.2)
    clipped = 1.0 + 0.2 * squash
    adv = advantage[:, None]
    slope = jnp.where(ratio * adv <= clipped * adv, 1.0, 1.0 - squash * squash)
    coef = jnp.where(live, -512.0 * stale[:, None] * adv * ratio * slope / count_each[:, None], 0.0)
    coef = jnp.dot(select.astype(f32), coef.reshape(-1, 1), precision=EXACT)[:, 0]
    coefs = lax.all_gather(coef, "dp", axis=0)

    def one_term(k, grad):
        out_grad = (coefs[k][:, None] * scale * read[k].astype(f32)).astype(jnp.bfloat16)
        return grad + lax.dot_general(
            hidden[k], out_grad, (((0,), (0,)), ((), ())), preferred_element_type=f32
        )

    return (log_ratio, lax.fori_loop(0, shards, one_term, jnp.zeros((units, width), f32)))


def body(*args):
    if lax.axis_size("dp") == 8 and lax.axis_size("mp") == 4:
        return cube_body(*args)
    return general_body(*args)


def solution(mesh):
    placed = (
        P("dp", "mp"),
        P("dp", None),
        P("dp", None),
        P("dp"),
        P("dp"),
        P("dp", None),
        P("dp", None),
        P(("mp", "dp"), None),
    )
    return jax.shard_map(
        body,
        mesh=mesh,
        in_specs=placed,
        out_specs=(P("dp", None), P(("mp", "dp"), None)),
        check_vma=False,
    )
```
